128 devices in a mesh: dp: 32 (over z, y, core), seq: 4 (over x).
Axes of the slice: x: 4, y: 4, z: 4, core: 2. Of those that a mesh axis runs over, the one named last changes fastest.
Arguments:
- frames: bfloat16 [768, 64, 1536], P('seq', 'dp'), may hold values from -6 to 6
- lengths: int32 [64], P('dp'), may hold values from 96 to 768, as said below
- attn_gain: float32 [1536], replicated, may hold values from 0.5 to 1.5
- w_qkv: bfloat16 [3, 1536, 1536], P(None, 'dp', 'seq'), may hold values from -2 to 2
- w_out: bfloat16 [1536, 1536], P('seq', 'dp'), may hold values from -0.15625 to 0.15625
- conv_gain: float32 [1536], replicated, may hold values from 0.5 to 1.5
- w_pw1: bfloat16 [1536, 3072], P(('dp', 'seq')), may hold values from -0.15625 to 0.15625
- depth_kernel: float32 [31, 1536], replicated, may hold values from -1 to 1
- mid_gain: float32 [1536], replicated, may hold values from 0.5 to 1.5
- w_pw2: bfloat16 [1536, 1536], P(('dp', 'seq')), may hold values from -0.15625 to 0.15625
Outputs:
- layer_out: bfloat16 [768, 64, 1536], P('seq', 'dp')
The draws below stay inside these ranges and needn't reach their ends.
Inputs may be any that keep to these rules, and one draw needn't show every extreme that they name: `lengths`: some utterance has exactly 768 valid frames.
All inputs are finite; a program needn't handle non-finite values.
Results may differ from the reference program's by a relative error of at most 0.018.
Values may be sent and summed in bfloat16 or wider, within the bound.
A program may use at most 128 MiB of HBM per device.

```python
import jax
import jax.numpy as jnp
from jax import lax

D = 1536
HD = 64
HEADS = 24
KERNEL = 31
HALO = 15
MAXLEN = 768
UTT = 64


def draw_lengths(key, part):
    key = jax.random.fold_in(key, 11)
    drawn = jax.random.randint(key, (UTT,), MAXLEN // 8, MAXLEN + 1).astype(jnp.int32)
    longest = jax.random.randint(jax.random.fold_in(key, 1), (), 0, UTT)
    return jnp.where(jnp.arange(UTT) == longest, MAXLEN, drawn).astype(jnp.int32)


def draw_w_qkv(key, part):
    key = jax.random.fold_in(key, 7)
    drawn = jax.random.normal(key, (3, D, D), jnp.float32) * D ** (-0.5)
    return jnp.clip(drawn, -2.0, 2.0).astype(jnp.bfloat16)


def levels(stream_key, extent, cuts, smallest, largest):
    factor_of = 1.0
    for axis_at, shards_of in cuts:
        heights = jax.random.uniform(jax.random.fold_in(jax.random.fold_in(stream_key, 6), axis_at), (shards_of,), jnp.float32, smallest / len(cuts), largest / len(cuts))
        factor_of = factor_of * jnp.repeat(jnp.exp(heights), extent[axis_at] // shards_of).reshape((-1,) + (1,) * (len(extent) - 1 - axis_at))
    return factor_of


def bell_draw(rng, shape, scale, most, pieces=(), kind=jnp.bfloat16):
    loudness = levels(rng, shape, pieces, -0.22, 0.18) if pieces else 1.0
    values = jax.random.normal(rng, shape, jnp.float32) * scale * loudness
    return jnp.minimum(jnp.maximum(values, -most), most).astype(kind)


def setup_inputs(seed: int = 0) -> dict:
    seeds = jax.random.split(jax.random.key(seed), 11)
    return {
        "frames": bell_draw(seeds[0], (MAXLEN, UTT, D), 1.0, 6.0, ((0, 4), (1, 32))),
        "lengths": draw_lengths(jax.random.fold_in(seeds[10], 71), 0),
        "attn_gain": jnp.clip(1.0 + 0.1 * jax.random.normal(seeds[2], (D,), jnp.float32), 0.5, 1.5),
        "w_qkv": draw_w_qkv(jax.random.fold_in(seeds[10], 71), 0),
        "w_out": bell_draw(seeds[4], (D, D), D ** -0.5, 0.15625, ((0, 4), (1, 32))),
        "conv_gain": jnp.clip(1.0 + 0.1 * jax.random.normal(seeds[5], (D,), jnp.float32), 0.5, 1.5),
        "w_pw1": bell_draw(seeds[6], (D, 2 * D), D ** -0.5, 0.15625, ((0, 128),)),
        "depth_kernel": bell_draw(seeds[7], (KERNEL, D), KERNEL ** -0.5, 1.0, (), jnp.float32),
        "mid_gain": jnp.clip(1.0 + 0.1 * jax.random.normal(seeds[8], (D,), jnp.float32), 0.5, 1.5),
        "w_pw2": bell_draw(seeds[9], (D, D), D ** -0.5, 0.15625, ((0, 128),)),
    }


def layer_norm(values, gain):
    average = lax.optimization_barrier(jnp.mean(values, -1, keepdims=True))
    centred = values - average
    spread = lax.optimization_barrier(jnp.mean(centred * centred, -1, keepdims=True))
    return centred * lax.rsqrt(spread + 1e-05) * gain

def reference(frames, lengths, attn_gain, w_qkv, w_out, conv_gain, w_pw1, depth_kernel, mid_gain, w_pw2):

    def one_utterance(operands):
        frame_rows, length = operands
        inside = lax.iota(jnp.int32, MAXLEN) < length
        normed = layer_norm(frame_rows.astype(jnp.float32), attn_gain).astype(jnp.bfloat16)
        queries = jnp.dot(normed, w_qkv[0], preferred_element_type=jnp.float32).astype(jnp.bfloat16)
        key_rows = jnp.dot(normed, w_qkv[1], preferred_element_type=jnp.float32).astype(jnp.bfloat16)
        value_rows = jnp.dot(normed, w_qkv[2], preferred_element_type=jnp.float32).astype(jnp.bfloat16)

        def heads_of(matrix):
            return matrix.reshape(MAXLEN, HEADS, HD).astype(jnp.float32)
        scores = jnp.einsum('qhd,khd->hqk', heads_of(queries), heads_of(key_rows)) * HD ** (-0.5)
        scores = jnp.where(inside[None, None, :], scores, -jnp.inf)
        weights = jax.nn.softmax(scores, axis=-1).astype(jnp.bfloat16)
        context = jnp.einsum('hqk,khd->qhd', weights.astype(jnp.float32), heads_of(value_rows))
        context = context.reshape(MAXLEN, D).astype(jnp.bfloat16)
        attended = jnp.dot(context, w_out, preferred_element_type=jnp.float32)
        residual = (frame_rows.astype(jnp.float32) + attended).astype(jnp.bfloat16)
        conv_in = layer_norm(residual.astype(jnp.float32), conv_gain).astype(jnp.bfloat16)
        projection = jnp.dot(conv_in, w_pw1, preferred_element_type=jnp.float32)
        gated = projection[:, :D] * jax.nn.sigmoid(projection[:, D:])
        gated = jnp.where(inside[:, None], gated, 0.0).astype(jnp.bfloat16)
        widened = jnp.pad(gated.astype(jnp.float32), ((HALO, HALO), (0, 0)))
        depthwise = jnp.zeros((MAXLEN, D), jnp.float32)
        for kernel_tap in range(KERNEL):
            depthwise = depthwise + widened[kernel_tap:kernel_tap + MAXLEN] * depth_kernel[kernel_tap]
        hidden = layer_norm(depthwise, mid_gain)
        activated = (hidden * jax.nn.sigmoid(hidden)).astype(jnp.bfloat16)
        projected = jnp.dot(activated, w_pw2, preferred_element_type=jnp.float32)
        result = jnp.where(inside[:, None], residual.astype(jnp.float32) + projected, 0.0)
        return result.astype(jnp.bfloat16)
    outputs = lax.map(one_utterance, (jnp.swapaxes(frames, 0, 1), lengths))
    return jnp.swapaxes(outputs, 0, 1)
```

```python
import functools

import jax
import jax.numpy as jnp
from jax import lax
from jax.experimental import pallas as pl
from jax.experimental.pallas import tpu as pltpu
from jax.sharding import PartitionSpec as P

HD = 64
KERNEL = 31
D = 1536
T = 768
L = 192
EDGE = 16
BF = jnp.bfloat16
F32 = jnp.float32
SCALE = 1.4426950408889634 / 8.0
NSEM = 96
ROWS = 32


def sigmoid(v):
    return 0.5 * jnp.tanh(0.5 * v) + 0.5


def norm_rows(v, gain):
    mean = jnp.mean(v, -1, keepdims=True)
    centred = v - mean
    spread = jnp.mean(centred * centred, -1, keepdims=True)
    return centred * lax.rsqrt(spread + 1e-05) * gain


def chunks(buf, lanes, first=0, count=32, mat=None):
    out = []
    for i in range(first, first + count):
        z, y, c = i // 8, (i // 2) % 4, i % 2
        where = (c, z, y) if c == 0 else (c, y, z)
        if mat is not None:
            where = where + (mat,)
        out.append(buf[where + (slice(None), lanes)])
    return jnp.concatenate(out, axis=0)


def body(
    lens, frames, gain_a, w_qkv, w_out, gain_c, w_pw, taps, gain_m, out,
    bq, bo, b1, b2, xg, nrm, nsend, qkv, kbias, ctxl, ctx, res, cin, gp, cf, dep, send, recv,
):
    x = lax.axis_index("seq")
    dp = lax.axis_index("dp")
    z, y, c = lax.div(dp, 8), lax.rem(lax.div(dp, 2), 4), lax.rem(dp, 2)
    a, b = lax.div(x, 2), lax.rem(x, 2)

    def mod4(v):
        return lax.rem(v, 4)

    A = (1 - c) * y + c * z
    B = (1 - c) * z + c * y

    def dev(Bv, Av):
        return (1 - c) * (Bv * 8 + Av * 2) + c * (Av * 8 + Bv * 2 + 1)

    Ap, Am, Bp, Bm, Bf = mod4(A + 1), mod4(A + 3), mod4(B + 1), mod4(B + 3), mod4(B + 2)
    dAp, dAm, dBp, dBm = dev(B, Ap), dev(B, Am), dev(Bp, A), dev(Bm, A)
    sib = dp + 1 - 2 * c
    near, mate, far = 3 - x, x + 1 - 2 * b, mod4(x + 2)

    names = {}

    def rc(name, src, dst, to_dp, to_x):
        i = names.setdefault(name, len(names))
        return pltpu.make_async_remote_copy(
            src_ref=src, dst_ref=dst, send_sem=send.at[i], recv_sem=recv.at[i],
            device_id=(to_dp, to_x), device_id_type=pl.DeviceIdType.MESH,
        )

    barrier = pltpu.get_barrier_semaphore()
    peers = [(dp, mod4(x + d)) for d in (1, 2, 3)]
    peers += [(d, x) for d in (dAp, dAm, dBp, dBm, sib)]
    for peer in peers:
        pl.semaphore_signal(barrier, inc=1, device_id=peer, device_id_type=pl.DeviceIdType.MESH)

    class Ring:
        def __init__(self, key, buf, half):
            same = lambda n, ref, to: rc(key + n, ref, ref, to, x)
            lo, hi = pl.ds(0, half), pl.ds(half, half)
            mid = (slice(None),) * (len(buf.shape) - 4)
            self.p1 = [same("p1+", buf.at[c, B, A], dAp), same("p1-", buf.at[c, B, A], dAm)]
            self.r1 = [
                same("r1+", buf.at[(c, B, Am) + mid + (lo,)], dAp),
                same("r1-", buf.at[(c, B, Ap) + mid + (hi,)], dAm),
            ]
            self.p2 = [same("p2+", buf.at[c, B], dBp), same("p2-", buf.at[c, B], dBm)]
            self.r2 = [
                same("r2+", buf.at[c, Bm, pl.ds(0, 2)], dBp),
                same("r2-", buf.at[c, Bp, pl.ds(2, 2)], dBm),
            ]
            self.s = [same("s%d" % i, buf.at[c, v], sib) for i, v in enumerate((B, Bm, Bp, Bf))]
            self.sent = self.p1 + self.r1 + self.p2 + self.r2 + self.s

        def P1(self):
            self.p1[0].start()
            self.p1[1].start()

        def R1(self):
            for i in (0, 1):
                self.p1[i].wait_recv()
                self.r1[i].start()

        def P2(self):
            self.r1[0].wait_recv()
            self.r1[1].wait_recv()
            self.p2[0].start()
            self.p2[1].start()
            self.s[0].start()

        def R2(self):
            for i in (0, 1):
                self.p2[i].wait_recv()
                self.r2[i].start()
                self.s[1 + i].start()

        def F(self):
            self.r2[0].wait_recv()
            self.r2[1].wait_recv()
            self.s[3].start()

        def G(self):
            for copy in self.s:
                copy.wait_recv()

        def done(self):
            for copy in self.sent:
                copy.wait_send()

    Q, O = Ring("q", bq, 384), Ring("o", bo, 768)
    W1, W2 = Ring("v", b1, 1536), Ring("w", b2, 768)

    own_q = bq.at[c, B, A, :, :, pl.ds(pl.multiple_of(384 * a, 128), 384)]
    own_o = bo.at[c, B, A, :, pl.ds(pl.multiple_of(384 * x, 128), 384)]
    qx = rc("qx", own_q, own_q, dp, far)
    ox = [rc("ox%d" % d, own_o, own_o, dp, mod4(x + d)) for d in (1, 2, 3)]
    gx = [rc("gx%d" % d, xg.at[x], xg.at[x], dp, mod4(x + d)) for d in (1, 2, 3)]
    fn = rc("fn", nsend, nrm.at[x], dp, near)
    fm = rc("fm", nrm.at[x], nrm.at[x], dp, mate)
    fr = rc("fr", nrm.at[near], nrm.at[near], dp, mate)

    own_q[...] = w_qkv[...]
    own_o[...] = w_out[...]
    xg[x] = w_pw[...]
    pl.semaphore_wait(barrier, len(peers))
    qx.start()

    def normed(u, target):
        def step(i, carry):
            rows = pl.ds(pl.multiple_of(i * ROWS, ROWS), ROWS)
            v = norm_rows(frames[u, rows, :].astype(F32), gain_a[...])
            target[rows, :] = v.astype(BF)
            return carry

        lax.fori_loop(0, L // ROWS, step, 0)

    normed(1 - a, nsend)
    fn.start()
    normed(a, nrm.at[x])
    fm.start()
    for copy in ox:
        copy.start()
    for copy in gx:
        copy.start()

    qx.wait_recv()
    Q.P1()
    length = lens[a]
    keys = lax.broadcasted_iota(jnp.int32, (T, 128), 0)
    lane = lax.broadcasted_iota(jnp.int32, (T, 128), 1)
    kbias[...] = jnp.where((keys >= length) & (lane == 0), -1e30, 0.0).astype(BF)
    Q.R1()
    for copy in ox:
        copy.wait_recv()
    O.P1()
    Q.P2()
    fn.wait_recv()
    fr.start()
    for copy in gx:
        copy.wait_recv()

    r = lax.broadcasted_iota(jnp.int32, (48, 64), 0)
    k = lax.broadcasted_iota(jnp.int32, (48, 64), 1)
    pick = ((lax.shift_right_logical(k, 4) * 12 + (k & 15) == r) & ((k & 15) < 12)).astype(F32).astype(BF)
    for n in range(6):
        lanes = slice(768 * n, 768 * n + 768)
        rows = jnp.concatenate([xg[i, :, lanes] for i in range(4)], axis=0)
        rows = jnp.dot(pick, rows, preferred_element_type=F32).astype(BF)
        if n < 4:
            b1[c, B, A, :, lanes] = rows
        else:
            b2[c, B, A, :, 768 * (n - 4) : 768 * (n - 3)] = rows
    W1.P1()
    O.R1()
    Q.R2()
    O.P2()
    W1.R1()
    W2.P1()
    Q.F()
    W1.P2()
    W2.R1()
    Q.G()
    for copy in (fm, fr):
        copy.wait_recv()

    def project(i, carry):
        m, n = lax.div(i, 3), lax.rem(i, 3)
        lanes = pl.ds(pl.multiple_of(n * 256, 256), 256)
        factor = jnp.where(m == 0, SCALE, 1.0).astype(F32)
        w = chunks(bq, lanes, mat=m)
        for j in range(4):
            v = jnp.dot(nrm[j], w, preferred_element_type=F32)
            qkv[m, L * j : L * j + L, lanes] = (v * factor).astype(BF)
        return carry

    lax.fori_loop(0, 9, project, 0)
    O.R2()

    sends = []
    for g in (0, 1):
        cols = pl.ds(pl.multiple_of(384 * (b + 2 * g), 128), 384)
        for d in (1, 2, 3):
            to = mod4(x + d)
            sends.append(
                rc("c%d%d" % (g, d), ctxl.at[to, :, pl.ds(384 * g, 384)], ctx.at[a, :, cols], dp, to)
            )

    QT = 192
    half = lax.broadcasted_iota(jnp.int32, (QT, 128), 1) < HD

    def attend(p, carry):
        lanes = pl.ds(pl.multiple_of(p * 128, 128), 128)
        key = jnp.concatenate([qkv[1, :, lanes], kbias[...]], axis=1)
        value = jnp.concatenate([qkv[2, :, lanes], jnp.ones((T, 128), BF)], axis=1)

        def tile(j, carry):
            rows = pl.ds(pl.multiple_of(j * QT, QT), QT)
            q = qkv[0, rows, lanes]
            results = []
            for h in (0, 1):
                mine = jnp.where(half if h == 0 else ~half, q, jnp.zeros_like(q))
                query = jnp.concatenate([mine, jnp.ones((QT, 128), BF)], axis=1)
                s = lax.dot_general(
                    query, key, (((1,), (1,)), ((), ())), preferred_element_type=F32
                )
                e = jnp.exp2(s - jnp.max(s, -1, keepdims=True)).astype(BF)
                o = jnp.dot(e, value, preferred_element_type=F32)
                results.append(o[:, :128] / o[:, 128:])
            ctxl[j, :, lanes] = jnp.where(half, results[0], results[1]).astype(BF)
            return carry

        lax.fori_loop(0, 4, tile, 0)

        @pl.when(p == 1)
        def _():
            O.F()
            W1.R2()
            W2.P2()

        @pl.when(p == 2)
        def _():
            for copy in sends[:3]:
                copy.start()

        @pl.when(p == 4)
        def _():
            W1.F()

        return carry

    lax.fori_loop(0, 6, attend, 0)
    for copy in sends[3:]:
        copy.start()
    W2.R2()
    for g in (0, 1):
        cols = pl.ds(pl.multiple_of(384 * (b + 2 * g), 128), 384)
        ctx[a, :, cols] = ctxl[x, :, 384 * g : 384 * g + 384]
    O.G()
    for copy in sends:
        copy.wait_recv()

    for n in range(2):
        w = chunks(bo, slice(None), 16 * n, 16)
        for u in (0, 1):
            att = lax.dot_general(
                ctx[u], w, (((1,), (1,)), ((), ())), preferred_element_type=F32
            )
            cols = slice(768 * n, 768 * n + 768)
            res[u, :, cols] = (frames[u, :, cols].astype(F32) + att).astype(BF)

    def norm_conv(i, carry):
        u, rows = lax.div(i, L // ROWS), pl.ds(pl.multiple_of(lax.rem(i, L // ROWS) * ROWS, ROWS), ROWS)
        cin[u, rows, :] = norm_rows(res[u, rows, :].astype(F32), gain_c[...]).astype(BF)
        return carry

    lax.fori_loop(0, 2 * (L // ROWS), norm_conv, 0)
    W2.F()
    W1.G()
    time = x * L + lax.broadcasted_iota(jnp.int32, (L, 256), 0)

    def glu(n, carry):
        lanes = pl.ds(pl.multiple_of(n * 256, 256), 256)
        wv = chunks(b1, lanes)
        wg = chunks(b1, pl.ds(pl.multiple_of(n * 256 + D, 256), 256))
        for u in (0, 1):
            v = jnp.dot(cin[u], wv, preferred_element_type=F32)
            g = jnp.dot(cin[u], wg, preferred_element_type=F32)
            v = jnp.where(time < lens[u], v * sigmoid(g), 0.0)
            gp[u, EDGE : EDGE + L, lanes] = v.astype(BF)
        return carry

    lax.fori_loop(0, 6, glu, 0)
    hp = rc("h+", gp.at[:, pl.ds(L, EDGE)], gp.at[:, pl.ds(0, EDGE)], dp, mod4(x + 1))
    hm = rc("h-", gp.at[:, pl.ds(EDGE, EDGE)], gp.at[:, pl.ds(EDGE + L, EDGE)], dp, mod4(x + 3))
    hp.start()
    hm.start()
    W2.G()
    hp.wait_recv()
    hm.wait_recv()
    first = jnp.where(x == 0, 0.0, 1.0).astype(F32)
    last = jnp.where(x == 3, 0.0, 1.0).astype(F32)

    def conv(i, carry):
        u, n = lax.div(i, 12), lax.rem(i, 12)
        lanes = pl.ds(pl.multiple_of(n * 128, 128), 128)
        cf[0:EDGE, :] = gp[u, 0:EDGE, lanes].astype(F32) * first
        cf[EDGE : EDGE + L, :] = gp[u, EDGE : EDGE + L, lanes].astype(F32)
        cf[EDGE + L :, :] = gp[u, EDGE + L :, lanes].astype(F32) * last
        tap = taps[:, lanes]
        total = jnp.zeros((L, 128), F32)
        for k in range(KERNEL):
            total = total + cf[k + 1 : k + 1 + L, :] * tap[k : k + 1, :]
        dep[u, :, lanes] = total
        return carry

    lax.fori_loop(0, 24, conv, 0)

    def norm_mid(i, carry):
        u, rows = lax.div(i, L // ROWS), pl.ds(pl.multiple_of(lax.rem(i, L // ROWS) * ROWS, ROWS), ROWS)
        h = norm_rows(dep[u, rows, :], gain_m[...])
        cin[u, rows, :] = (h * sigmoid(h)).astype(BF)
        return carry

    lax.fori_loop(0, 2 * (L // ROWS), norm_mid, 0)

    def last_product(n, carry):
        lanes = pl.ds(pl.multiple_of(n * 256, 256), 256)
        w = chunks(b2, lanes)
        for u in (0, 1):
            v = jnp.dot(cin[u], w, preferred_element_type=F32) + res[u, :, lanes].astype(F32)
            out[u, :, lanes] = jnp.where(time < lens[u], v, 0.0).astype(BF)
        return carry

    lax.fori_loop(0, 6, last_product, 0)

    for ring in (Q, O, W1, W2):
        ring.done()
    for copy in [qx] + ox + gx + [fn, fm, fr] + sends + [hp, hm]:
        copy.wait_send()


def local(
    frames, lengths, attn_gain, w_qkv, w_out, conv_gain, w_pw1, depth_kernel, mid_gain, w_pw2
):
    rows = jnp.swapaxes(frames, 0, 1)
    pw = jnp.pad(jnp.concatenate([w_pw1, w_pw2], axis=1), ((0, 4), (0, 0)))
    vmem = pl.BlockSpec(memory_space=pltpu.VMEM)
    result = pl.pallas_call(
        body,
        out_shape=jax.ShapeDtypeStruct((2, L, D), BF),
        in_specs=[pl.BlockSpec(memory_space=pltpu.SMEM)] + [vmem] * 8,
        out_specs=vmem,
        scratch_shapes=[
            pltpu.VMEM((2, 4, 4, 3, 48, 768), BF),
            pltpu.VMEM((2, 4, 4, 48, D), BF),
            pltpu.VMEM((2, 4, 4, 48, 2 * D), BF),
            pltpu.VMEM((2, 4, 4, 48, D), BF),
            pltpu.VMEM((4, 16, 3 * D), BF),
            pltpu.VMEM((4, L, D), BF),
            pltpu.VMEM((L, D), BF),
            pltpu.VMEM((3, T, 768), BF),
            pltpu.VMEM((T, 128), BF),
            pltpu.VMEM((4, L, 768), BF),
            pltpu.VMEM((2, L, D), BF),
            pltpu.VMEM((2, L, D), BF),
            pltpu.VMEM((2, L, D), BF),
            pltpu.VMEM((2, L + 2 * EDGE, D), BF),
            pltpu.VMEM((L + 2 * EDGE, 128), F32),
            pltpu.VMEM((2, L, D), F32),
            pltpu.SemaphoreType.DMA((NSEM,)),
            pltpu.SemaphoreType.DMA((NSEM,)),
        ],
        compiler_params=pltpu.CompilerParams(
            collective_id=0, has_side_effects=True, vmem_limit_bytes=60 * 1024 * 1024
        ),
        name="layer",
    )(
        lengths, rows, attn_gain[None], w_qkv, w_out.T, conv_gain[None], pw, depth_kernel,
        mid_gain[None],
    )
    return jnp.swapaxes(result, 0, 1)


def solution(mesh):
    in_specs = (
        P("seq", "dp", None),
        P("dp"),
        P(),
        P(None, "dp", "seq"),
        P("seq", "dp"),
        P(),
        P(("dp", "seq"), None),
        P(),
        P(),
        P(("dp", "seq"), None),
    )
    out_specs = P("seq", "dp", None)
    return jax.shard_map(local, mesh=mesh, in_specs=in_specs, out_specs=out_specs, check_vma=False)
```

```python
import functools

import jax
import jax.numpy as jnp
from jax import lax
from jax.experimental import pallas as pl
from jax.experimental.pallas import tpu as pltpu
from jax.sharding import PartitionSpec as P

HD = 64
KERNEL = 31
D = 1536
T = 768
L = 192
EDGE = 16
BF = jnp.bfloat16
F32 = jnp.float32
SCALE = 1.4426950408889634 / 8.0
NSEM = 112
ROWS = 96


def sigmoid(v):
    return 0.5 * jnp.tanh(0.5 * v) + 0.5


def norm_rows(v, gain):
    mean = jnp.mean(v, -1, keepdims=True)
    centred = v - mean
    spread = jnp.mean(centred * centred, -1, keepdims=True)
    return centred * lax.rsqrt(spread + 1e-05) * gain


def chunks(buf, lanes, first=0, count=32, mat=None):
    out = []
    for i in range(first, first + count):
        z, y, c = i // 8, (i // 2) % 4, i % 2
        where = (c, z, y) if c == 0 else (c, y, z)
        if mat is not None:
            where = where + (mat,)
        out.append(buf[where + (slice(None), lanes)])
    return jnp.concatenate(out, axis=0)


def body(
    lens, frames, gain_a, w_qkv, w_out, gain_c, w_pw1, w_pw2, taps, gain_m, out,
    bq, bo, b1, b2, xg, nrm, nsend, qkv, kbias, ctxl, ctx, res, cin, gp, cf, dep, send, recv,
):
    x = lax.axis_index("seq")
    dp = lax.axis_index("dp")
    z, y, c = lax.div(dp, 8), lax.rem(lax.div(dp, 2), 4), lax.rem(dp, 2)

    def mod4(v):
        return lax.rem(v, 4)

    xc = mod4(x + c)
    a, b, hi = lax.div(xc, 2), lax.rem(x, 2), lax.div(x, 2)

    A = (1 - c) * y + c * z
    B = (1 - c) * z + c * y

    def dev(Bv, Av):
        return (1 - c) * (Bv * 8 + Av * 2) + c * (Av * 8 + Bv * 2 + 1)

    Ap, Am, Bp, Bm, Bf = mod4(A + 1), mod4(A + 3), mod4(B + 1), mod4(B + 3), mod4(B + 2)
    dAp, dAm, dBp, dBm = dev(B, Ap), dev(B, Am), dev(Bp, A), dev(Bm, A)
    dAf = dev(B, mod4(A + 2))
    sib = dp + 1 - 2 * c
    near, mate = mod4(7 - xc - c), mod4(xc + 5 - 2 * lax.rem(xc, 2) - c)
    far = mod4(x + 2)

    names = {}

    def rc(name, src, dst, to_dp, to_x):
        i = names.setdefault(name, len(names))
        return pltpu.make_async_remote_copy(
            src_ref=src, dst_ref=dst, send_sem=send.at[i], recv_sem=recv.at[i],
            device_id=(to_dp, to_x), device_id_type=pl.DeviceIdType.MESH,
        )

    barrier = pltpu.get_barrier_semaphore()
    peers = [(dp, mod4(x + d)) for d in (1, 2, 3)]
    peers += [(d, x) for d in (dAp, dAm, dAf, dBp, dBm, sib)]
    for peer in peers:
        pl.semaphore_signal(barrier, inc=1, device_id=peer, device_id_type=pl.DeviceIdType.MESH)

    class Ring:
        def __init__(self, key, buf, half, direct=False):
            same = lambda n, ref, to: rc(key + n, ref, ref, to, x)
            lo, hi_ = pl.ds(0, half), pl.ds(half, half)
            mid = (slice(None),) * (len(buf.shape) - 4)
            if direct:
                self.p1, self.r1 = [], []
                for n, v in (("own", hi), ("far", 1 - hi)):
                    at = pl.ds(pl.multiple_of(v * half, 128), half)
                    ref = buf.at[(c, B, A) + mid + (at,)]
                    for m, to in (("+", dAp), ("-", dAm), ("2", dAf)):
                        self.p1.append(same(n + m, ref, to))
            else:
                self.p1 = [same("p1+", buf.at[c, B, A], dAp), same("p1-", buf.at[c, B, A], dAm)]
                self.r1 = [
                    same("r1+", buf.at[(c, B, Am) + mid + (lo,)], dAp),
                    same("r1-", buf.at[(c, B, Ap) + mid + (hi_,)], dAm),
                ]
            first, second = pl.ds(0, 2), pl.ds(2, 2)
            self.p2 = [
                same("p2a+", buf.at[c, B, first], dBp), same("p2a-", buf.at[c, B, second], dBm),
                same("p2b+", buf.at[c, B, second], dBp), same("p2b-", buf.at[c, B, first], dBm),
            ]
            self.r2 = [
                same("r2+", buf.at[c, Bm, first], dBp), same("r2-", buf.at[c, Bp, second], dBm),
            ]
            self.s = [same("s%d" % i, buf.at[c, v], sib) for i, v in enumerate((B, Bm, Bp, Bf))]
            self.sent = self.p1 + self.r1 + self.p2 + self.r2 + self.s

        def P1(self, first=0, count=2):
            for copy in self.p1[first : first + count]:
                copy.start()

        def R1(self):
            for i in (0, 1):
                self.p1[i].wait_recv()
                self.r1[i].start()

        def P2(self):
            for copy in self.r1 or self.p1:
                copy.wait_recv()
            for copy in self.p2:
                copy.start()
            self.s[0].start()

        def R2(self):
            for i in (0, 1):
                self.p2[i].wait_recv()
                self.r2[i].start()

        def S2(self):
            for i in (0, 1):
                self.p2[2 + i].wait_recv()
                self.s[1 + i].start()

        def F(self):
            self.r2[0].wait_recv()
            self.r2[1].wait_recv()
            self.s[3].start()

        def G(self):
            for copy in self.s:
                copy.wait_recv()

        def done(self):
            for copy in self.sent:
                copy.wait_send()

    Q, O = Ring("q", bq, 384, True), Ring("o", bo, 768)
    W1, W2 = Ring("v", b1, 1536), Ring("w", b2, 768)

    own_q = bq.at[c, B, A, :, :, pl.ds(pl.multiple_of(384 * hi, 128), 384)]
    own_o = bo.at[c, B, A, :, pl.ds(pl.multiple_of(384 * x, 128), 384)]
    qx = rc("qx", own_q, own_q, dp, far)
    ox = [rc("ox%d" % d, own_o, own_o, dp, mod4(x + d)) for d in (1, 2, 3)]
    gx = [rc("gx%d" % d, xg.at[x], xg.at[x], dp, mod4(x + d)) for d in (1, 2, 3)]
    fn = rc("fn", nsend, nrm.at[x], dp, near)
    fm = rc("fm", nrm.at[x], nrm.at[x], dp, mate)
    fr = rc("fr", nrm.at[near], nrm.at[near], dp, mate)

    own_q[...] = w_qkv[...]
    own_o[...] = w_out[...]
    xg[x] = jnp.zeros((16, 3 * D), BF)
    xg[x, 0:12, 0 : 2 * D] = w_pw1[...]
    xg[x, 0:12, 2 * D :] = w_pw2[...]
    pl.semaphore_wait(barrier, len(peers))
    qx.start()
    Q.P1(0, 3)
    for copy in ox + gx:
        copy.start()

    def normed(u, target):
        def step(i, carry):
            rows = pl.ds(pl.multiple_of(i * ROWS, ROWS), ROWS)
            v = norm_rows(frames[u, rows, :].astype(F32), gain_a[...][None])
            target[rows, :] = v.astype(BF)
            return carry

        lax.fori_loop(0, L // ROWS, step, 0)

    normed(1 - a, nsend)
    fn.start()
    normed(a, nrm.at[x])
    fm.start()
    qx.wait_recv()
    Q.P1(3, 3)
    length = lens[a]
    keys = lax.broadcasted_iota(jnp.int32, (T, 128), 0)
    lane = lax.broadcasted_iota(jnp.int32, (T, 128), 1)
    kbias[...] = jnp.where((keys >= length) & (lane == 0), -1e30, 0.0).astype(BF)
    for copy in ox:
        copy.wait_recv()
    O.P1()
    Q.P2()
    fn.wait_recv()
    fr.start()
    O.R1()
    for copy in gx:
        copy.wait_recv()

    r = lax.broadcasted_iota(jnp.int32, (48, 64), 0)
    k = lax.broadcasted_iota(jnp.int32, (48, 64), 1)
    pick = ((lax.shift_right_logical(k, 4) * 12 + (k & 15) == r) & ((k & 15) < 12)).astype(F32).astype(BF)
    for n in range(6):
        lanes = slice(768 * n, 768 * n + 768)
        rows = jnp.concatenate([xg[i, :, lanes] for i in range(4)], axis=0)
        rows = jnp.dot(pick, rows, preferred_element_type=F32).astype(BF)
        if n < 4:
            b1[c, B, A, :, lanes] = rows
        else:
            b2[c, B, A, :, 768 * (n - 4) : 768 * (n - 3)] = rows
    Q.R2()
    W1.P1()
    W2.P1()
    O.P2()
    Q.S2()
    Q.F()
    Q.G()
    for copy in (fm, fr):
        copy.wait_recv()

    def project(i, carry):
        m, n = lax.div(i, 3), lax.rem(i, 3)
        lanes = pl.ds(pl.multiple_of(n * 256, 256), 256)
        factor = jnp.where(m == 0, SCALE, 1.0).astype(F32)
        w = chunks(bq, lanes, mat=m)
        for j in range(4):
            v = jnp.dot(nrm[j], w, preferred_element_type=F32)
            qkv[m, L * j : L * j + L, lanes] = (v * factor).astype(BF)

        @pl.when(i == 4)
        def _():
            W1.R1()
            W2.R1()

        return carry

    lax.fori_loop(0, 9, project, 0)
    O.R2()

    def send_pair(p, d):
        to = mod4(x + d)
        block = b + 2 * lax.div(p, 3)
        cols = pl.ds(pl.multiple_of(384 * block + 128 * lax.rem(p, 3), 128), 128)
        i = 80 + 3 * p + d - 1
        return pltpu.make_async_remote_copy(
            src_ref=ctxl.at[to, :, pl.ds(pl.multiple_of(p * 128, 128), 128)],
            dst_ref=ctx.at[a, :, cols], send_sem=send.at[i], recv_sem=recv.at[i],
            device_id=(dp, to), device_id_type=pl.DeviceIdType.MESH,
        )

    QT = 192
    half = lax.broadcasted_iota(jnp.int32, (QT, 128), 1) < HD

    def attend(p, carry):
        lanes = pl.ds(pl.multiple_of(p * 128, 128), 128)
        key = jnp.concatenate([qkv[1, :, lanes], kbias[...]], axis=1)
        value = jnp.concatenate([qkv[2, :, lanes], jnp.ones((T, 128), BF)], axis=1)

        def tile(j, carry):
            rows = pl.ds(pl.multiple_of(j * QT, QT), QT)
            q = qkv[0, rows, lanes]
            results = []
            for h in (0, 1):
                mine = jnp.where(half if h == 0 else ~half, q, jnp.zeros_like(q))
                query = jnp.concatenate([mine, jnp.ones((QT, 128), BF)], axis=1)
                s = lax.dot_general(
                    query, key, (((1,), (1,)), ((), ())), preferred_element_type=F32
                )
                e = jnp.exp2(s - jnp.max(s, -1, keepdims=True)).astype(BF)
                o = jnp.dot(e, value, preferred_element_type=F32)
                results.append(o[:, :128] / o[:, 128:])
            ctxl[j, :, lanes] = jnp.where(half, results[0], results[1]).astype(BF)
            return carry

        lax.fori_loop(0, 4, tile, 0, unroll=4)

        for d in (2, 1, 3):
            send_pair(p, d).start()

        @pl.when(p == 1)
        def _():
            W1.P2()
            O.S2()
            O.F()

        @pl.when(p == 4)
        def _():
            W1.R2()
            W2.P2()

        return carry

    lax.fori_loop(0, 6, attend, 0)
    for g in (0, 1):
        cols = pl.ds(pl.multiple_of(384 * (b + 2 * g), 128), 384)
        ctx[a, :, cols] = ctxl[x, :, 384 * g : 384 * g + 384]
    O.G()

    def arrive(p, carry):
        for d in (1, 2, 3):
            send_pair(p, d).wait_recv()
        return carry

    lax.fori_loop(0, 6, arrive, 0)

    for n in range(2):
        w = chunks(bo, slice(None), 16 * n, 16)
        for u in (0, 1):
            att = lax.dot_general(
                ctx[u], w, (((1,), (1,)), ((), ())), preferred_element_type=F32
            )
            cols = slice(768 * n, 768 * n + 768)
            res[u, :, cols] = (frames[u, :, cols].astype(F32) + att).astype(BF)

    def norm_conv(i, carry):
        u, rows = lax.div(i, L // ROWS), pl.ds(pl.multiple_of(lax.rem(i, L // ROWS) * ROWS, ROWS), ROWS)
        cin[u, rows, :] = norm_rows(res[u, rows, :].astype(F32), gain_c[...][None]).astype(BF)
        return carry

    lax.fori_loop(0, 2 * (L // ROWS), norm_conv, 0)
    W1.S2()
    W1.F()
    W1.G()
    time = x * L + lax.broadcasted_iota(jnp.int32, (L, 256), 0)

    def glu(n, carry):
        lanes = pl.ds(pl.multiple_of(n * 256, 256), 256)
        wv = chunks(b1, lanes)
        wg = chunks(b1, pl.ds(pl.multiple_of(n * 256 + D, 256), 256))
        for u in (0, 1):
            v = jnp.dot(cin[u], wv, preferred_element_type=F32)
            g = jnp.dot(cin[u], wg, preferred_element_type=F32)
            v = jnp.where(time < lens[u], v * sigmoid(g), 0.0)
            gp[u, EDGE : EDGE + L, lanes] = v.astype(BF)

        @pl.when(n == 2)
        def _():
            W2.R2()

        return carry

    lax.fori_loop(0, 6, glu, 0)
    hp = rc("h+", gp.at[:, pl.ds(L, EDGE)], gp.at[:, pl.ds(0, EDGE)], dp, mod4(x + 1))
    hm = rc("h-", gp.at[:, pl.ds(EDGE, EDGE)], gp.at[:, pl.ds(EDGE + L, EDGE)], dp, mod4(x + 3))
    hp.start()
    hm.start()
    W2.S2()
    hp.wait_recv()
    hm.wait_recv()
    first = jnp.where(x == 0, 0.0, 1.0).astype(F32)
    last = jnp.where(x == 3, 0.0, 1.0).astype(F32)

    def conv(i, carry):
        u, n = lax.div(i, 12), lax.rem(i, 12)
        lanes = pl.ds(pl.multiple_of(n * 128, 128), 128)
        cf[0:EDGE, :] = gp[u, 0:EDGE, lanes].astype(F32) * first
        cf[EDGE : EDGE + L, :] = gp[u, EDGE : EDGE + L, lanes].astype(F32)
        cf[EDGE + L :, :] = gp[u, EDGE + L :, lanes].astype(F32) * last
        tap = taps[:, lanes]
        total = jnp.zeros((L, 128), F32)
        for k in range(KERNEL):
            total = total + cf[k + 1 : k + 1 + L, :] * tap[k : k + 1, :]
        dep[u, :, lanes] = total
        return carry

    lax.fori_loop(0, 24, conv, 0)
    W2.F()

    def norm_mid(i, carry):
        u, rows = lax.div(i, L // ROWS), pl.ds(pl.multiple_of(lax.rem(i, L // ROWS) * ROWS, ROWS), ROWS)
        h = norm_rows(dep[u, rows, :], gain_m[...][None])
        cin[u, rows, :] = (h * sigmoid(h)).astype(BF)
        return carry

    lax.fori_loop(0, 2 * (L // ROWS), norm_mid, 0)

    W2.G()

    def last_product(n, carry):
        lanes = pl.ds(pl.multiple_of(n * 256, 256), 256)
        w = chunks(b2, lanes)
        for u in (0, 1):
            v = jnp.dot(cin[u], w, preferred_element_type=F32) + res[u, :, lanes].astype(F32)
            out[u, :, lanes] = jnp.where(time < lens[u], v, 0.0).astype(BF)
        return carry

    lax.fori_loop(0, 6, last_product, 0)

    for ring in (Q, O, W1, W2):
        ring.done()
    for copy in [qx] + ox + gx + [fn, fm, fr, hp, hm]:
        copy.wait_send()

    def leave(p, carry):
        for d in (1, 2, 3):
            send_pair(p, d).wait_send()
        return carry

    lax.fori_loop(0, 6, leave, 0)


def local(
    frames, lengths, attn_gain, w_qkv, w_out, conv_gain, w_pw1, depth_kernel, mid_gain, w_pw2
):
    rows = jnp.swapaxes(frames, 0, 1)
    vmem = pl.BlockSpec(memory_space=pltpu.VMEM)
    result = pl.pallas_call(
        body,
        out_shape=jax.ShapeDtypeStruct((2, L, D), BF),
        in_specs=[pl.BlockSpec(memory_space=pltpu.SMEM)] + [vmem] * 9,
        out_specs=vmem,
        scratch_shapes=[
            pltpu.VMEM((2, 4, 4, 3, 48, 768), BF),
            pltpu.VMEM((2, 4, 4, 48, D), BF),
            pltpu.VMEM((2, 4, 4, 48, 2 * D), BF),
            pltpu.VMEM((2, 4, 4, 48, D), BF),
            pltpu.VMEM((4, 16, 3 * D), BF),
            pltpu.VMEM((4, L, D), BF),
            pltpu.VMEM((L, D), BF),
            pltpu.VMEM((3, T, 768), BF),
            pltpu.VMEM((T, 128), BF),
            pltpu.VMEM((4, L, 768), BF),
            pltpu.VMEM((2, L, D), BF),
            pltpu.VMEM((2, L, D), BF),
            pltpu.VMEM((2, L, D), BF),
            pltpu.VMEM((2, L + 2 * EDGE, D), BF),
            pltpu.VMEM((L + 2 * EDGE, 128), F32),
            pltpu.VMEM((2, L, D), F32),
            pltpu.SemaphoreType.DMA((NSEM,)),
            pltpu.SemaphoreType.DMA((NSEM,)),
        ],
        compiler_params=pltpu.CompilerParams(
            collective_id=0, has_side_effects=True, vmem_limit_bytes=60 * 1024 * 1024
        ),
        name="layer",
    )(
        lengths, rows, attn_gain, w_qkv, w_out.T, conv_gain, w_pw1, w_pw2, depth_kernel, mid_gain,
    )
    return jnp.swapaxes(result, 0, 1)


def solution(mesh):
    in_specs = (
        P("seq", "dp", None),
        P("dp"),
        P(),
        P(None, "dp", "seq"),
        P("seq", "dp"),
        P(),
        P(("dp", "seq"), None),
        P(),
        P(),
        P(("dp", "seq"), None),
    )
    out_specs = P("seq", "dp", None)
    return jax.shard_map(local, mesh=mesh, in_specs=in_specs, out_specs=out_specs, check_vma=False)
```

```python
import functools

import jax
import jax.numpy as jnp
from jax import lax
from jax.experimental import pallas as pl
from jax.experimental.pallas import tpu as pltpu
from jax.sharding import PartitionSpec as P

HD = 64
KERNEL = 31
D = 1536
T = 768
L = 192
EDGE = 16
BF = jnp.bfloat16
F32 = jnp.float32
SCALE = 1.4426950408889634 / 8.0
NSEM = 112
QT = 384
ROWS = 192


def sigmoid(v):
    return 0.5 * jnp.tanh(0.5 * v) + 0.5


def norm_rows(v, gain):
    mean = jnp.mean(v, -1, keepdims=True)
    centred = v - mean
    spread = jnp.mean(centred * centred, -1, keepdims=True)
    return centred * lax.rsqrt(spread + 1e-05) * gain


def chunks(buf, lanes, first=0, count=32, mat=None):
    out = []
    for i in range(first, first + count):
        z, y, c = i // 8, (i // 2) % 4, i % 2
        where = (c, z, y) if c == 0 else (c, y, z)
        if mat is not None:
            where = (mat[0],) + where + (mat[1],)
        out.append(buf[where + (slice(None), lanes)])
    return jnp.concatenate(out, axis=0)


def body(
    lens, frames, gain_a, w_qkv, w_out, gain_c, w_pw1, w_pw2, taps, gain_m, out,
    bq, bo, b1, b2, xg, nrm, nsend, qkv, kbias, ctxl, ctx, res, cin, gp, cf, dep, send, recv,
):
    x = lax.axis_index("seq")
    dp = lax.axis_index("dp")
    z, y, c = lax.div(dp, 8), lax.rem(lax.div(dp, 2), 4), lax.rem(dp, 2)

    def mod4(v):
        return lax.rem(v, 4)

    xc = mod4(x + c)
    a = lax.div(xc, 2)

    A = (1 - c) * y + c * z
    B = (1 - c) * z + c * y

    def dev(Bv, Av):
        return (1 - c) * (Bv * 8 + Av * 2) + c * (Av * 8 + Bv * 2 + 1)

    Ap, Am, Bp, Bm, Bf = mod4(A + 1), mod4(A + 3), mod4(B + 1), mod4(B + 3), mod4(B + 2)
    dAp, dAm, dBp, dBm = dev(B, Ap), dev(B, Am), dev(Bp, A), dev(Bm, A)
    dAf = dev(B, mod4(A + 2))
    sib = dp + 1 - 2 * c
    near, mate = mod4(7 - xc - c), mod4(xc + 5 - 2 * lax.rem(xc, 2) - c)
    far = mod4(x + 2)

    names = {}

    def rc(name, src, dst, to_dp, to_x):
        i = names.setdefault(name, len(names))
        return pltpu.make_async_remote_copy(
            src_ref=src, dst_ref=dst, send_sem=send.at[i], recv_sem=recv.at[i],
            device_id=(to_dp, to_x), device_id_type=pl.DeviceIdType.MESH,
        )

    barrier = pltpu.get_barrier_semaphore()
    peers = [(dp, mod4(x + d)) for d in (1, 2, 3)]
    peers += [(d, x) for d in (dAp, dAm, dAf, dBp, dBm, sib)]
    for peer in peers:
        pl.semaphore_signal(barrier, inc=1, device_id=peer, device_id_type=pl.DeviceIdType.MESH)

    class Ring:
        def __init__(self, key, buf, half, direct=False):
            same = lambda n, ref, to: rc(key + n, ref, ref, to, x)
            lo, hi_ = pl.ds(0, half), pl.ds(half, half)
            mid = (slice(None),) * (len(buf.shape) - 4)
            if direct:
                self.r1 = []
                self.p1 = [
                    same("p1" + m, buf.at[c, B, A], to)
                    for m, to in (("+", dAp), ("-", dAm), ("2", dAf))
                ]
            else:
                self.p1 = [same("p1+", buf.at[c, B, A], dAp), same("p1-", buf.at[c, B, A], dAm)]
                self.r1 = [
                    same("r1+", buf.at[(c, B, Am) + mid + (lo,)], dAp),
                    same("r1-", buf.at[(c, B, Ap) + mid + (hi_,)], dAm),
                ]
            first, second = pl.ds(0, 2), pl.ds(2, 2)
            self.p2 = [
                same("p2a+", buf.at[c, B, first], dBp), same("p2a-", buf.at[c, B, second], dBm),
                same("p2b+", buf.at[c, B, second], dBp), same("p2b-", buf.at[c, B, first], dBm),
            ]
            self.r2 = [
                same("r2+", buf.at[c, Bm, first], dBp), same("r2-", buf.at[c, Bp, second], dBm),
            ]
            self.s = [same("s%d" % i, buf.at[c, v], sib) for i, v in enumerate((B, Bm, Bp, Bf))]
            self.sent = self.p1 + self.r1 + self.p2 + self.r2 + self.s

        def P1(self):
            for copy in self.p1:
                copy.start()

        def R1(self):
            for i in (0, 1):
                self.p1[i].wait_recv()
                self.r1[i].start()

        def P2(self):
            for copy in self.r1 or self.p1:
                copy.wait_recv()
            for copy in self.p2:
                copy.start()
            self.s[0].start()

        def R2(self):
            for i in (0, 1):
                self.p2[i].wait_recv()
                self.r2[i].start()

        def S2(self):
            for i in (0, 1):
                self.p2[2 + i].wait_recv()
                self.s[1 + i].start()

        def F(self):
            self.r2[0].wait_recv()
            self.r2[1].wait_recv()
            self.s[3].start()

        def G(self):
            for copy in self.s:
                copy.wait_recv()

        def done(self):
            for copy in self.sent:
                copy.wait_send()

    QA, QB = Ring("q", bq.at[0], 0, True), Ring("r", bq.at[1], 0, True)
    O = Ring("o", bo, 768)
    W1, W2 = Ring("v", b1, 1536), Ring("w", b2, 768)

    own_q = bq.at[0, c, B, A]
    own_o = bo.at[c, B, A, :, pl.ds(pl.multiple_of(384 * x, 128), 384)]
    qx = rc("qx", own_q, bq.at[1, c, B, A], dp, far)
    ox = [rc("ox%d" % d, own_o, own_o, dp, mod4(x + d)) for d in (1, 2, 3)]
    parts = [xg.at[x, :, pl.ds(0, 2 * D)], xg.at[x, :, pl.ds(2 * D, D)]]
    g1 = [rc("g1%d" % d, parts[0], parts[0], dp, mod4(x + d)) for d in (1, 2, 3)]
    g2 = [rc("g2%d" % d, parts[1], parts[1], dp, mod4(x + d)) for d in (1, 2, 3)]
    fn = rc("fn", nsend, nrm.at[x], dp, near)
    fm = rc("fm", nrm.at[x], nrm.at[x], dp, mate)
    fr = rc("fr", nrm.at[near], nrm.at[near], dp, mate)

    own_q[...] = w_qkv[...]
    own_o[...] = w_out[...]
    xg[x] = jnp.zeros((16, 3 * D), BF)
    xg[x, 0:12, 0 : 2 * D] = w_pw1[...]
    xg[x, 0:12, 2 * D :] = w_pw2[...]
    pl.semaphore_wait(barrier, len(peers))
    qx.start()
    QA.P1()
    for copy in ox + g1:
        copy.start()

    def normed(u, target):
        def step(i, carry):
            rows = pl.ds(pl.multiple_of(i * ROWS, ROWS), ROWS)
            v = norm_rows(frames[u, rows, :].astype(F32), gain_a[...][None])
            target[rows, :] = v.astype(BF)
            return carry

        lax.fori_loop(0, L // ROWS, step, 0)

    normed(1 - a, nsend)
    fn.start()
    normed(a, nrm.at[x])
    fm.start()
    QA.P2()
    qx.wait_recv()
    QB.P1()
    length = lens[a]
    keys = lax.broadcasted_iota(jnp.int32, (T, 128), 0)
    lane = lax.broadcasted_iota(jnp.int32, (T, 128), 1)
    kbias[...] = jnp.where((keys >= length) & (lane == 0), -1e30, 0.0).astype(BF)
    QA.R2()
    QB.P2()
    for copy in ox:
        copy.wait_recv()
    O.P1()
    QA.S2()
    QB.R2()
    for copy in g1:
        copy.wait_recv()

    r = lax.broadcasted_iota(jnp.int32, (48, 64), 0)
    k = lax.broadcasted_iota(jnp.int32, (48, 64), 1)
    pick = ((lax.shift_right_logical(k, 4) * 12 + (k & 15) == r) & ((k & 15) < 12)).astype(F32).astype(BF)

    def assemble(first, count, target):
        for n in range(count):
            lanes = slice(768 * (first + n), 768 * (first + n) + 768)
            rows = jnp.concatenate([xg[i, :, lanes] for i in range(4)], axis=0)
            rows = jnp.dot(pick, rows, preferred_element_type=F32).astype(BF)
            target[c, B, A, :, 768 * n : 768 * n + 768] = rows

    assemble(0, 4, b1)
    W1.P1()
    O.R1()
    fn.wait_recv()
    fr.start()
    for copy in g2:
        copy.start()
    QA.F()
    O.P2()
    W1.R1()
    QB.S2()
    QB.F()
    QA.G()
    for copy in (fm, fr):
        copy.wait_recv()

    def project(g):
        def step(m, carry):
            factor = jnp.where(m == 0, SCALE, 1.0).astype(F32)
            w = chunks(bq, slice(None), mat=(g, m))
            v = jnp.dot(nrm[...].reshape(T, D), w, preferred_element_type=F32)
            qkv[m, :, 384 * g : 384 * g + 384] = (v * factor).astype(BF)
            return carry

        lax.fori_loop(0, 3, step, 0)

    project(0)
    for copy in g2:
        copy.wait_recv()
    assemble(4, 2, b2)
    W2.P1()
    O.R2()
    W1.P2()

    def send_pair(p, d):
        to = mod4(x + d)
        block = mod4(x + 2 * lax.div(p, 3))
        cols = pl.ds(pl.multiple_of(384 * block + 128 * lax.rem(p, 3), 128), 128)
        i = 94 + 3 * p + d - 1
        return pltpu.make_async_remote_copy(
            src_ref=ctxl.at[pl.ds(pl.multiple_of(to * L, L), L), pl.ds(pl.multiple_of(p * 128, 128), 128)],
            dst_ref=ctx.at[a, :, cols], send_sem=send.at[i], recv_sem=recv.at[i],
            device_id=(dp, to), device_id_type=pl.DeviceIdType.MESH,
        )

    half = lax.broadcasted_iota(jnp.int32, (QT, 128), 1) < HD

    def attend(p, carry):
        lanes = pl.ds(pl.multiple_of(p * 128, 128), 128)
        key = jnp.concatenate([qkv[1, :, lanes], kbias[...]], axis=1)
        value = jnp.concatenate([qkv[2, :, lanes], jnp.ones((T, 128), BF)], axis=1)

        def tile(j, carry):
            rows = pl.ds(pl.multiple_of(j * QT, QT), QT)
            q = qkv[0, rows, lanes]
            results = []
            for h in (0, 1):
                mine = jnp.where(half if h == 0 else ~half, q, jnp.zeros_like(q))
                query = jnp.concatenate([mine, jnp.ones((QT, 128), BF)], axis=1)
                s = lax.dot_general(
                    query, key, (((1,), (1,)), ((), ())), preferred_element_type=F32
                )
                e = jnp.exp2(s - jnp.max(s, -1, keepdims=True)).astype(BF)
                o = jnp.dot(e, value, preferred_element_type=F32)
                results.append(o[:, :128] / o[:, 128:])
            ctxl[rows, lanes] = jnp.where(half, results[0], results[1]).astype(BF)
            return carry

        lax.fori_loop(0, T // QT, tile, 0, unroll=T // QT)

        for d in (2, 1, 3):
            send_pair(p, d).start()

        @pl.when(p == 0)
        def _():
            W2.R1()

        @pl.when(p == 2)
        def _():
            O.S2()
            O.F()

        @pl.when(p == 3)
        def _():
            W1.R2()
            W2.P2()

        return carry

    lax.fori_loop(0, 3, attend, 0)
    QB.G()
    project(1)
    lax.fori_loop(3, 6, attend, 0)
    for g in (0, 1):
        cols = pl.ds(pl.multiple_of(384 * mod4(x + 2 * g), 128), 384)
        ctx[a, :, cols] = ctxl[pl.ds(pl.multiple_of(x * L, L), L), 384 * g : 384 * g + 384]
    O.G()

    def arrive(p, carry):
        for d in (1, 2, 3):
            send_pair(p, d).wait_recv()
        return carry

    lax.fori_loop(0, 6, arrive, 0)

    for n in range(2):
        w = chunks(bo, slice(None), 16 * n, 16)
        cols = slice(768 * n, 768 * n + 768)
        att = lax.dot_general(
            ctx[...].reshape(2 * L, D), w, (((1,), (1,)), ((), ())), preferred_element_type=F32
        )
        total = frames[:, :, cols].astype(F32) + att.reshape(2, L, 768)
        res[:, :, cols] = total.astype(BF)

    def norm_conv(i, carry):
        u, rows = lax.div(i, L // ROWS), pl.ds(pl.multiple_of(lax.rem(i, L // ROWS) * ROWS, ROWS), ROWS)
        cin[u, rows, :] = norm_rows(res[u, rows, :].astype(F32), gain_c[...][None]).astype(BF)
        return carry

    lax.fori_loop(0, 2 * (L // ROWS), norm_conv, 0)
    W1.S2()
    W1.F()
    W1.G()
    time = x * L + lax.broadcasted_iota(jnp.int32, (L, 256), 0)

    def glu(n, carry):
        lanes = pl.ds(pl.multiple_of(n * 256, 256), 256)
        wv = chunks(b1, lanes)
        wg = chunks(b1, pl.ds(pl.multiple_of(n * 256 + D, 256), 256))
        rows = cin[...].reshape(2 * L, D)
        v = jnp.dot(rows, wv, preferred_element_type=F32)
        g = jnp.dot(rows, wg, preferred_element_type=F32)
        v = (v * sigmoid(g)).reshape(2, L, 256)
        for u in (0, 1):
            gp[u, EDGE : EDGE + L, lanes] = jnp.where(time < lens[u], v[u], 0.0).astype(BF)

        @pl.when(n == 2)
        def _():
            W2.R2()

        return carry

    lax.fori_loop(0, 6, glu, 0)
    hp = rc("h+", gp.at[:, pl.ds(L, EDGE)], gp.at[:, pl.ds(0, EDGE)], dp, mod4(x + 1))
    hm = rc("h-", gp.at[:, pl.ds(EDGE, EDGE)], gp.at[:, pl.ds(EDGE + L, EDGE)], dp, mod4(x + 3))
    hp.start()
    hm.start()
    W2.S2()
    hp.wait_recv()
    hm.wait_recv()
    first = jnp.where(x == 0, 0.0, 1.0).astype(F32)
    last = jnp.where(x == 3, 0.0, 1.0).astype(F32)

    def conv(i, carry):
        u, n = lax.div(i, 12), lax.rem(i, 12)
        lanes = pl.ds(pl.multiple_of(n * 128, 128), 128)
        cf[0:EDGE, :] = gp[u, 0:EDGE, lanes].astype(F32) * first
        cf[EDGE : EDGE + L, :] = gp[u, EDGE : EDGE + L, lanes].astype(F32)
        cf[EDGE + L :, :] = gp[u, EDGE + L :, lanes].astype(F32) * last
        tap = taps[:, lanes]
        total = jnp.zeros((L, 128), F32)
        for k in range(KERNEL):
            total = total + cf[k + 1 : k + 1 + L, :] * tap[k : k + 1, :]
        dep[u, :, lanes] = total
        return carry

    lax.fori_loop(0, 24, conv, 0)
    W2.F()

    def norm_mid(i, carry):
        u, rows = lax.div(i, L // ROWS), pl.ds(pl.multiple_of(lax.rem(i, L // ROWS) * ROWS, ROWS), ROWS)
        h = norm_rows(dep[u, rows, :], gain_m[...][None])
        cin[u, rows, :] = (h * sigmoid(h)).astype(BF)
        return carry

    lax.fori_loop(0, 2 * (L // ROWS), norm_mid, 0)

    W2.G()

    def last_product(n, carry):
        lanes = pl.ds(pl.multiple_of(n * 256, 256), 256)
        w = chunks(b2, lanes)
        v = jnp.dot(cin[...].reshape(2 * L, D), w, preferred_element_type=F32).reshape(2, L, 256)
        for u in (0, 1):
            total = v[u] + res[u, :, lanes].astype(F32)
            out[u, :, lanes] = jnp.where(time < lens[u], total, 0.0).astype(BF)
        return carry

    lax.fori_loop(0, 6, last_product, 0)

    for ring in (QA, QB, O, W1, W2):
        ring.done()
    for copy in [qx] + ox + g1 + g2 + [fn, fm, fr, hp, hm]:
        copy.wait_send()

    def leave(p, carry):
        for d in (1, 2, 3):
            send_pair(p, d).wait_send()
        return carry

    lax.fori_loop(0, 6, leave, 0)


def local(
    frames, lengths, attn_gain, w_qkv, w_out, conv_gain, w_pw1, depth_kernel, mid_gain, w_pw2
):
    rows = jnp.swapaxes(frames, 0, 1)
    vmem = pl.BlockSpec(memory_space=pltpu.VMEM)
    result = pl.pallas_call(
        body,
        out_shape=jax.ShapeDtypeStruct((2, L, D), BF),
        in_specs=[pl.BlockSpec(memory_space=pltpu.SMEM)] + [vmem] * 9,
        out_specs=vmem,
        scratch_shapes=[
            pltpu.VMEM((2, 2, 4, 4, 3, 48, 384), BF),
            pltpu.VMEM((2, 4, 4, 48, D), BF),
            pltpu.VMEM((2, 4, 4, 48, 2 * D), BF),
            pltpu.VMEM((2, 4, 4, 48, D), BF),
            pltpu.VMEM((4, 16, 3 * D), BF),
            pltpu.VMEM((4, L, D), BF),
            pltpu.VMEM((L, D), BF),
            pltpu.VMEM((3, T, 768), BF),
            pltpu.VMEM((T, 128), BF),
            pltpu.VMEM((T, 768), BF),
            pltpu.VMEM((2, L, D), BF),
            pltpu.VMEM((2, L, D), BF),
            pltpu.VMEM((2, L, D), BF),
            pltpu.VMEM((2, L + 2 * EDGE, D), BF),
            pltpu.VMEM((L + 2 * EDGE, 128), F32),
            pltpu.VMEM((2, L, D), F32),
            pltpu.SemaphoreType.DMA((NSEM,)),
            pltpu.SemaphoreType.DMA((NSEM,)),
        ],
        compiler_params=pltpu.CompilerParams(
            collective_id=0, has_side_effects=True, vmem_limit_bytes=60 * 1024 * 1024
        ),
        name="layer",
    )(
        lengths, rows, attn_gain, w_qkv, w_out.T, conv_gain, w_pw1, w_pw2, depth_kernel, mid_gain,
    )
    return jnp.swapaxes(result, 0, 1)


def solution(mesh):
    in_specs = (
        P("seq", "dp", None),
        P("dp"),
        P(),
        P(None, "dp", "seq"),
        P("seq", "dp"),
        P(),
        P(("dp", "seq"), None),
        P(),
        P(),
        P(("dp", "seq"), None),
    )
    out_specs = P("seq", "dp", None)
    return jax.shard_map(local, mesh=mesh, in_specs=in_specs, out_specs=out_specs, check_vma=False)
```

```python
import functools

import jax
import jax.numpy as jnp
from jax import lax
from jax.experimental import pallas as pl
from jax.experimental.pallas import tpu as pltpu
from jax.sharding import PartitionSpec as P

HD = 64
KERNEL = 31
D = 1536
T = 768
L = 192
EDGE = 16
BF = jnp.bfloat16
F32 = jnp.float32
SCALE = 1.4426950408889634 / 8.0
NSEM = 112
QT = 384
ROWS = 192


def sigmoid(v):
    return 0.5 * jnp.tanh(0.5 * v) + 0.5


def norm_rows(v, gain):
    mean = jnp.mean(v, -1, keepdims=True)
    centred = v - mean
    spread = jnp.mean(centred * centred, -1, keepdims=True)
    return centred * lax.rsqrt(spread + 1e-05) * gain


def chunks(buf, lanes, first=0, count=32, mat=None):
    out = []
    for i in range(first, first + count):
        z, y, c = i // 8, (i // 2) % 4, i % 2
        where = (c, z, y) if c == 0 else (c, y, z)
        if mat is not None:
            where = (mat[0],) + where + (mat[1],)
        out.append(buf[where + (slice(None), lanes)])
    return jnp.concatenate(out, axis=0)


def body(
    lens, frames, gain_a, w_qkv, w_out, gain_c, w_pw1, w_pw2, taps, gain_m, out,
    bq, bo, b1, b2, xg, nrm, nsend, qkv, kbias, ctxl, ctx, res, cin, gp, cf, dep, send, recv,
):
    x = lax.axis_index("seq")
    dp = lax.axis_index("dp")
    z, y, c = lax.div(dp, 8), lax.rem(lax.div(dp, 2), 4), lax.rem(dp, 2)

    def mod4(v):
        return lax.rem(v, 4)

    xc = mod4(x + c)
    a = lax.div(xc, 2)

    A = (1 - c) * y + c * z
    B = (1 - c) * z + c * y

    def dev(Bv, Av):
        return (1 - c) * (Bv * 8 + Av * 2) + c * (Av * 8 + Bv * 2 + 1)

    Ap, Am, Bp, Bm, Bf = mod4(A + 1), mod4(A + 3), mod4(B + 1), mod4(B + 3), mod4(B + 2)
    dAp, dAm, dBp, dBm = dev(B, Ap), dev(B, Am), dev(Bp, A), dev(Bm, A)
    dAf = dev(B, mod4(A + 2))
    sib = dp + 1 - 2 * c
    near, mate = mod4(7 - xc - c), mod4(xc + 5 - 2 * lax.rem(xc, 2) - c)
    far = mod4(x + 2)

    names = {}

    def rc(name, src, dst, to_dp, to_x):
        i = names.setdefault(name, len(names))
        return pltpu.make_async_remote_copy(
            src_ref=src, dst_ref=dst, send_sem=send.at[i], recv_sem=recv.at[i],
            device_id=(to_dp, to_x), device_id_type=pl.DeviceIdType.MESH,
        )

    barrier = pltpu.get_barrier_semaphore()
    peers = [(dp, mod4(x + d)) for d in (1, 2, 3)]
    peers += [(d, x) for d in (dAp, dAm, dAf, dBp, dBm, sib)]
    for peer in peers:
        pl.semaphore_signal(barrier, inc=1, device_id=peer, device_id_type=pl.DeviceIdType.MESH)

    class Ring:
        def __init__(self, key, buf, half, direct=False):
            same = lambda n, ref, to: rc(key + n, ref, ref, to, x)
            lo, hi_ = pl.ds(0, half), pl.ds(half, half)
            mid = (slice(None),) * (len(buf.shape) - 4)
            if direct:
                self.r1 = []
                self.p1 = [
                    same("p1" + m, buf.at[c, B, A], to)
                    for m, to in (("+", dAp), ("-", dAm), ("2", dAf))
                ]
            else:
                self.p1 = [same("p1+", buf.at[c, B, A], dAp), same("p1-", buf.at[c, B, A], dAm)]
                self.r1 = [
                    same("r1+", buf.at[(c, B, Am) + mid + (lo,)], dAp),
                    same("r1-", buf.at[(c, B, Ap) + mid + (hi_,)], dAm),
                ]
            first, second = pl.ds(0, 2), pl.ds(2, 2)
            self.p2 = [
                same("p2a+", buf.at[c, B, first], dBp), same("p2a-", buf.at[c, B, second], dBm),
                same("p2b+", buf.at[c, B, second], dBp), same("p2b-", buf.at[c, B, first], dBm),
            ]
            self.r2 = [
                same("r2+", buf.at[c, Bm, first], dBp), same("r2-", buf.at[c, Bp, second], dBm),
            ]
            self.s = [same("s%d" % i, buf.at[c, v], sib) for i, v in enumerate((B, Bm, Bp, Bf))]
            self.sent = self.p1 + self.r1 + self.p2 + self.r2 + self.s

        def P1(self):
            for copy in self.p1:
                copy.start()

        def R1(self):
            for i in (0, 1):
                self.p1[i].wait_recv()
                self.r1[i].start()

        def P2(self):
            for copy in self.r1 or self.p1:
                copy.wait_recv()
            for copy in self.p2:
                copy.start()
            self.s[0].start()

        def R2(self):
            for i in (0, 1):
                self.p2[i].wait_recv()
                self.r2[i].start()

        def S2(self):
            for i in (0, 1):
                self.p2[2 + i].wait_recv()
                self.s[1 + i].start()

        def F(self):
            self.r2[0].wait_recv()
            self.r2[1].wait_recv()
            self.s[3].start()

        def G(self):
            for copy in self.s:
                copy.wait_recv()

        def done(self):
            for copy in self.sent:
                copy.wait_send()

    QA, QB = Ring("q", bq.at[0], 0, True), Ring("r", bq.at[1], 0, True)
    O = Ring("o", bo, 768)
    W1, W2 = Ring("v", b1, 1536), Ring("w", b2, 768)

    own_q = bq.at[0, c, B, A]
    own_o = bo.at[c, B, A, :, pl.ds(pl.multiple_of(384 * x, 128), 384)]
    qx = rc("qx", own_q, bq.at[1, c, B, A], dp, far)
    ox = [rc("ox%d" % d, own_o, own_o, dp, mod4(x + d)) for d in (1, 2, 3)]
    parts = [xg.at[x, :, pl.ds(0, 2 * D)], xg.at[x, :, pl.ds(2 * D, D)]]
    g1 = [rc("g1%d" % d, parts[0], parts[0], dp, mod4(x + d)) for d in (1, 2, 3)]
    g2 = [rc("g2%d" % d, parts[1], parts[1], dp, mod4(x + d)) for d in (1, 2, 3)]
    fn = rc("fn", nsend, nrm.at[x], dp, near)
    fm = rc("fm", nrm.at[x], nrm.at[x], dp, mate)
    fr = rc("fr", nrm.at[near], nrm.at[near], dp, mate)

    own_q[...] = w_qkv[...]
    own_o[...] = w_out[...]
    xg[x] = jnp.zeros((16, 3 * D), BF)
    xg[x, 0:12, 0 : 2 * D] = w_pw1[...]
    xg[x, 0:12, 2 * D :] = w_pw2[...]
    pl.semaphore_wait(barrier, len(peers))
    qx.start()
    QA.P1()
    for copy in ox + g1:
        copy.start()

    def normed(u, target):
        def step(i, carry):
            rows = pl.ds(pl.multiple_of(i * ROWS, ROWS), ROWS)
            v = norm_rows(frames[u, rows, :].astype(F32), gain_a[...][None])
            target[rows, :] = v.astype(BF)
            return carry

        lax.fori_loop(0, L // ROWS, step, 0)

    normed(1 - a, nsend)
    fn.start()
    normed(a, nrm.at[x])
    fm.start()
    QA.P2()
    qx.wait_recv()
    QB.P1()
    length = lens[a]
    keys = lax.broadcasted_iota(jnp.int32, (T, 128), 0)
    lane = lax.broadcasted_iota(jnp.int32, (T, 128), 1)
    kbias[...] = jnp.where((keys >= length) & (lane == 0), -1e30, 0.0).astype(BF)
    QA.R2()
    QB.P2()
    for copy in ox:
        copy.wait_recv()
    O.P1()
    QA.S2()
    QB.R2()
    for copy in g1:
        copy.wait_recv()

    r = lax.broadcasted_iota(jnp.int32, (48, 64), 0)
    k = lax.broadcasted_iota(jnp.int32, (48, 64), 1)
    pick = ((lax.shift_right_logical(k, 4) * 12 + (k & 15) == r) & ((k & 15) < 12)).astype(F32).astype(BF)

    def assemble(first, count, target):
        for n in range(count):
            lanes = slice(768 * (first + n), 768 * (first + n) + 768)
            rows = jnp.concatenate([xg[i, :, lanes] for i in range(4)], axis=0)
            rows = jnp.dot(pick, rows, preferred_element_type=F32).astype(BF)
            target[c, B, A, :, 768 * n : 768 * n + 768] = rows

    assemble(0, 4, b1)
    W1.P1()
    O.R1()
    QA.F()
    QA.G()
    fn.wait_recv()
    fr.start()
    for copy in g2:
        copy.start()
    fm.wait_recv()

    def project(g, blocks):
        def step(m, carry):
            factor = jnp.where(m == 0, SCALE, 1.0).astype(F32)
            w = chunks(bq, slice(None), mat=(g, m))
            for j in blocks:
                rows = pl.ds(pl.multiple_of(j * L, 64), L)
                v = jnp.dot(nrm[j], w, preferred_element_type=F32)
                qkv[m, rows, 384 * g : 384 * g + 384] = (v * factor).astype(BF)
            return carry

        lax.fori_loop(0, 3, step, 0)

    project(0, (x, mate, near))
    QB.S2()
    QB.F()
    W1.R1()
    O.P2()
    QB.G()
    project(1, (x, mate, near))
    O.R2()
    W1.P2()
    fr.wait_recv()
    project(0, (far,))
    project(1, (far,))
    for copy in g2:
        copy.wait_recv()
    assemble(4, 2, b2)
    W2.P1()

    def send_pair(p, d):
        to = mod4(x + d)
        block = mod4(x + 2 * lax.div(p, 3))
        cols = pl.ds(pl.multiple_of(384 * block + 128 * lax.rem(p, 3), 128), 128)
        i = 94 + 3 * p + d - 1
        return pltpu.make_async_remote_copy(
            src_ref=ctxl.at[pl.ds(pl.multiple_of(to * L, L), L), pl.ds(pl.multiple_of(p * 128, 128), 128)],
            dst_ref=ctx.at[a, :, cols], send_sem=send.at[i], recv_sem=recv.at[i],
            device_id=(dp, to), device_id_type=pl.DeviceIdType.MESH,
        )

    half = lax.broadcasted_iota(jnp.int32, (QT, 128), 1) < HD

    def attend(p, carry):
        lanes = pl.ds(pl.multiple_of(p * 128, 128), 128)
        key = jnp.concatenate([qkv[1, :, lanes], kbias[...]], axis=1)
        value = jnp.concatenate([qkv[2, :, lanes], jnp.ones((T, 128), BF)], axis=1)

        def tile(j, carry):
            rows = pl.ds(pl.multiple_of(j * QT, QT), QT)
            q = qkv[0, rows, lanes]
            results = []
            for h in (0, 1):
                mine = jnp.where(half if h == 0 else ~half, q, jnp.zeros_like(q))
                query = jnp.concatenate([mine, jnp.ones((QT, 128), BF)], axis=1)
                s = lax.dot_general(
                    query, key, (((1,), (1,)), ((), ())), preferred_element_type=F32
                )
                e = jnp.exp2(s - jnp.max(s, -1, keepdims=True)).astype(BF)
                o = jnp.dot(e, value, preferred_element_type=F32)
                results.append(o[:, :128] / o[:, 128:])
            ctxl[rows, lanes] = jnp.where(half, results[0], results[1]).astype(BF)
            return carry

        lax.fori_loop(0, T // QT, tile, 0, unroll=T // QT)

        for d in (2, 1, 3):
            send_pair(p, d).start()

        @pl.when(p == 4)
        def _():
            W1.R2()
            O.S2()

        return carry

    lax.fori_loop(0, 6, attend, 0)
    O.F()
    W2.R1()
    for g in (0, 1):
        cols = pl.ds(pl.multiple_of(384 * mod4(x + 2 * g), 128), 384)
        ctx[a, :, cols] = ctxl[pl.ds(pl.multiple_of(x * L, L), L), 384 * g : 384 * g + 384]
    O.G()

    def arrive(p, carry):
        for d in (1, 2, 3):
            send_pair(p, d).wait_recv()
        return carry

    lax.fori_loop(0, 6, arrive, 0)

    for n in range(2):
        w = chunks(bo, slice(None), 16 * n, 16)
        cols = slice(768 * n, 768 * n + 768)
        att = lax.dot_general(
            ctx[...].reshape(2 * L, D), w, (((1,), (1,)), ((), ())), preferred_element_type=F32
        )
        total = frames[:, :, cols].astype(F32) + att.reshape(2, L, 768)
        res[:, :, cols] = total.astype(BF)

    def norm_conv(i, carry):
        u, rows = lax.div(i, L // ROWS), pl.ds(pl.multiple_of(lax.rem(i, L // ROWS) * ROWS, ROWS), ROWS)
        cin[u, rows, :] = norm_rows(res[u, rows, :].astype(F32), gain_c[...][None]).astype(BF)
        return carry

    lax.fori_loop(0, 2 * (L // ROWS), norm_conv, 0)
    W1.S2()
    W2.P2()
    W1.F()
    W1.G()
    time = x * L + lax.broadcasted_iota(jnp.int32, (L, 256), 0)

    halo = []
    for v in (0, 1):
        at = lambda row: gp.at[:, pl.ds(row, EDGE), pl.ds(768 * v, 768)]
        halo.append(rc("h+%d" % v, at(L), at(0), dp, mod4(x + 1)))
        halo.append(rc("h-%d" % v, at(EDGE), at(EDGE + L), dp, mod4(x + 3)))

    def glu(n, carry):
        lanes = pl.ds(pl.multiple_of(n * 256, 256), 256)
        wv = chunks(b1, lanes)
        wg = chunks(b1, pl.ds(pl.multiple_of(n * 256 + D, 256), 256))
        rows = cin[...].reshape(2 * L, D)
        v = jnp.dot(rows, wv, preferred_element_type=F32)
        g = jnp.dot(rows, wg, preferred_element_type=F32)
        v = (v * sigmoid(g)).reshape(2, L, 256)
        for u in (0, 1):
            gp[u, EDGE : EDGE + L, lanes] = jnp.where(time < lens[u], v[u], 0.0).astype(BF)

        @pl.when(n == 2)
        def _():
            halo[0].start()
            halo[1].start()

        @pl.when(n == 4)
        def _():
            W2.R2()

        return carry

    lax.fori_loop(0, 6, glu, 0)
    halo[2].start()
    halo[3].start()
    W2.S2()
    halo[0].wait_recv()
    halo[1].wait_recv()
    first = jnp.where(x == 0, 0.0, 1.0).astype(F32)
    last = jnp.where(x == 3, 0.0, 1.0).astype(F32)

    def conv(i, carry):
        u, n = lax.rem(i, 2), lax.div(i, 2)
        lanes = pl.ds(pl.multiple_of(n * 128, 128), 128)
        cf[0:EDGE, :] = gp[u, 0:EDGE, lanes].astype(F32) * first
        cf[EDGE : EDGE + L, :] = gp[u, EDGE : EDGE + L, lanes].astype(F32)
        cf[EDGE + L :, :] = gp[u, EDGE + L :, lanes].astype(F32) * last
        tap = taps[:, lanes]
        total = jnp.zeros((L, 128), F32)
        for k in range(KERNEL):
            total = total + cf[k + 1 : k + 1 + L, :] * tap[k : k + 1, :]
        dep[u, :, lanes] = total
        return carry

    lax.fori_loop(0, 12, conv, 0)
    halo[2].wait_recv()
    halo[3].wait_recv()
    lax.fori_loop(12, 24, conv, 0)
    W2.F()

    def norm_mid(i, carry):
        u, rows = lax.div(i, L // ROWS), pl.ds(pl.multiple_of(lax.rem(i, L // ROWS) * ROWS, ROWS), ROWS)
        h = norm_rows(dep[u, rows, :], gain_m[...][None])
        cin[u, rows, :] = (h * sigmoid(h)).astype(BF)
        return carry

    lax.fori_loop(0, 2 * (L // ROWS), norm_mid, 0)

    W2.G()

    def last_product(n, carry):
        lanes = pl.ds(pl.multiple_of(n * 256, 256), 256)
        w = chunks(b2, lanes)
        v = jnp.dot(cin[...].reshape(2 * L, D), w, preferred_element_type=F32).reshape(2, L, 256)
        for u in (0, 1):
            total = v[u] + res[u, :, lanes].astype(F32)
            out[u, :, lanes] = jnp.where(time < lens[u], total, 0.0).astype(BF)
        return carry

    lax.fori_loop(0, 6, last_product, 0)

    for ring in (QA, QB, O, W1, W2):
        ring.done()
    for copy in [qx] + ox + g1 + g2 + [fn, fm, fr] + halo:
        copy.wait_send()

    def leave(p, carry):
        for d in (1, 2, 3):
            send_pair(p, d).wait_send()
        return carry

    lax.fori_loop(0, 6, leave, 0)


def local(
    frames, lengths, attn_gain, w_qkv, w_out, conv_gain, w_pw1, depth_kernel, mid_gain, w_pw2
):
    rows = jnp.swapaxes(frames, 0, 1)
    vmem = pl.BlockSpec(memory_space=pltpu.VMEM)
    result = pl.pallas_call(
        body,
        out_shape=jax.ShapeDtypeStruct((2, L, D), BF),
        in_specs=[pl.BlockSpec(memory_space=pltpu.SMEM)] + [vmem] * 9,
        out_specs=vmem,
        scratch_shapes=[
            pltpu.VMEM((2, 2, 4, 4, 3, 48, 384), BF),
            pltpu.VMEM((2, 4, 4, 48, D), BF),
            pltpu.VMEM((2, 4, 4, 48, 2 * D), BF),
            pltpu.VMEM((2, 4, 4, 48, D), BF),
            pltpu.VMEM((4, 16, 3 * D), BF),
            pltpu.VMEM((4, L, D), BF),
            pltpu.VMEM((L, D), BF),
            pltpu.VMEM((3, T, 768), BF),
            pltpu.VMEM((T, 128), BF),
            pltpu.VMEM((T, 768), BF),
            pltpu.VMEM((2, L, D), BF),
            pltpu.VMEM((2, L, D), BF),
            pltpu.VMEM((2, L, D), BF),
            pltpu.VMEM((2, L + 2 * EDGE, D), BF),
            pltpu.VMEM((L + 2 * EDGE, 128), F32),
            pltpu.VMEM((2, L, D), F32),
            pltpu.SemaphoreType.DMA((NSEM,)),
            pltpu.SemaphoreType.DMA((NSEM,)),
        ],
        compiler_params=pltpu.CompilerParams(
            collective_id=0, has_side_effects=True, vmem_limit_bytes=60 * 1024 * 1024
        ),
        name="layer",
    )(
        lengths, rows, attn_gain, w_qkv, w_out.T, conv_gain, w_pw1, w_pw2, depth_kernel, mid_gain,
    )
    return jnp.swapaxes(result, 0, 1)


def solution(mesh):
    in_specs = (
        P("seq", "dp", None),
        P("dp"),
        P(),
        P(None, "dp", "seq"),
        P("seq", "dp"),
        P(),
        P(("dp", "seq"), None),
        P(),
        P(),
        P(("dp", "seq"), None),
    )
    out_specs = P("seq", "dp", None)
    return jax.shard_map(local, mesh=mesh, in_specs=in_specs, out_specs=out_specs, check_vma=False)
```

```python
import functools

import jax
import jax.numpy as jnp
from jax import lax
from jax.experimental import pallas as pl
from jax.experimental.pallas import tpu as pltpu
from jax.sharding import PartitionSpec as P

HD = 64
KERNEL = 31
D = 1536
T = 768
L = 192
EDGE = 16
BF = jnp.bfloat16
F32 = jnp.float32
SCALE = 1.4426950408889634 / 8.0
NSEM = 112
QT = 384
ROWS = 192


def sigmoid(v):
    return 0.5 * jnp.tanh(0.5 * v) + 0.5


def norm_rows(v, gain):
    mean = jnp.mean(v, -1, keepdims=True)
    centred = v - mean
    spread = jnp.mean(centred * centred, -1, keepdims=True)
    return centred * lax.rsqrt(spread + 1e-05) * gain


def chunks(buf, lanes, first=0, count=32, mat=None):
    out = []
    for i in range(first, first + count):
        z, y, c = i // 8, (i // 2) % 4, i % 2
        where = (c, z, y) if c == 0 else (c, y, z)
        if mat is not None:
            where = (mat[0],) + where + (mat[1],)
        out.append(buf[where + (slice(None), lanes)])
    return jnp.concatenate(out, axis=0)


def body(
    lens, raw, gain_a, w_qkv, w_out, gain_c, w_pw1, w_pw2, taps, gain_m, out,
    bq, bo, b1, b2, xg, nrm, nsend, qkv, kbias, ctxl, ctx, res, cin, gp, cf, dep, frames, send, recv,
):
    x = lax.axis_index("seq")
    dp = lax.axis_index("dp")
    z, y, c = lax.div(dp, 8), lax.rem(lax.div(dp, 2), 4), lax.rem(dp, 2)

    def mod4(v):
        return lax.rem(v, 4)

    xc = mod4(x + c)
    a = lax.div(xc, 2)

    A = (1 - c) * y + c * z
    B = (1 - c) * z + c * y

    def dev(Bv, Av):
        return (1 - c) * (Bv * 8 + Av * 2) + c * (Av * 8 + Bv * 2 + 1)

    Ap, Am, Bp, Bm, Bf = mod4(A + 1), mod4(A + 3), mod4(B + 1), mod4(B + 3), mod4(B + 2)
    dAp, dAm, dBp, dBm = dev(B, Ap), dev(B, Am), dev(Bp, A), dev(Bm, A)
    dAf = dev(B, mod4(A + 2))
    sib = dp + 1 - 2 * c
    near, mate = mod4(7 - xc - c), mod4(xc + 5 - 2 * lax.rem(xc, 2) - c)
    far = mod4(x + 2)

    names = {}

    def rc(name, src, dst, to_dp, to_x):
        i = names.setdefault(name, len(names))
        return pltpu.make_async_remote_copy(
            src_ref=src, dst_ref=dst, send_sem=send.at[i], recv_sem=recv.at[i],
            device_id=(to_dp, to_x), device_id_type=pl.DeviceIdType.MESH,
        )

    barrier = pltpu.get_barrier_semaphore()
    peers = [(dp, mod4(x + d)) for d in (1, 2, 3)]
    peers += [(d, x) for d in (dAp, dAm, dAf, dBp, dBm, sib)]
    for peer in peers:
        pl.semaphore_signal(barrier, inc=1, device_id=peer, device_id_type=pl.DeviceIdType.MESH)

    class Ring:
        def __init__(self, key, buf, half, direct=False):
            same = lambda n, ref, to: rc(key + n, ref, ref, to, x)
            lo, hi_ = pl.ds(0, half), pl.ds(half, half)
            mid = (slice(None),) * (len(buf.shape) - 4)
            if direct:
                self.r1 = []
                self.p1 = [
                    same("p1" + m, buf.at[c, B, A], to)
                    for m, to in (("+", dAp), ("-", dAm), ("2", dAf))
                ]
            else:
                self.p1 = [same("p1+", buf.at[c, B, A], dAp), same("p1-", buf.at[c, B, A], dAm)]
                self.r1 = [
                    same("r1+", buf.at[(c, B, Am) + mid + (lo,)], dAp),
                    same("r1-", buf.at[(c, B, Ap) + mid + (hi_,)], dAm),
                ]
            first, second = pl.ds(0, 2), pl.ds(2, 2)
            self.p2 = [
                same("p2a+", buf.at[c, B, first], dBp), same("p2a-", buf.at[c, B, second], dBm),
                same("p2b+", buf.at[c, B, second], dBp), same("p2b-", buf.at[c, B, first], dBm),
            ]
            self.r2 = [
                same("r2+", buf.at[c, Bm, first], dBp), same("r2-", buf.at[c, Bp, second], dBm),
            ]
            self.s = [same("s%d" % i, buf.at[c, v], sib) for i, v in enumerate((B, Bm, Bp, Bf))]
            self.sent = self.p1 + self.r1 + self.p2 + self.r2 + self.s

        def P1(self):
            for copy in self.p1:
                copy.start()

        def R1(self):
            for i in (0, 1):
                self.p1[i].wait_recv()
                self.r1[i].start()

        def P2(self):
            for copy in self.r1 or self.p1:
                copy.wait_recv()
            for copy in self.p2:
                copy.start()
            self.s[0].start()

        def R2(self):
            for i in (0, 1):
                self.p2[i].wait_recv()
                self.r2[i].start()

        def S2(self):
            for i in (0, 1):
                self.p2[2 + i].wait_recv()
                self.s[1 + i].start()

        def F(self):
            self.r2[0].wait_recv()
            self.r2[1].wait_recv()
            self.s[3].start()

        def G(self):
            for copy in self.s:
                copy.wait_recv()

        def done(self):
            for copy in self.sent:
                copy.wait_send()

    QA, QB = Ring("q", bq.at[0], 0, True), Ring("r", bq.at[1], 0, True)
    O = Ring("o", bo, 768)
    W1, W2 = Ring("v", b1, 1536), Ring("w", b2, 768)

    own_q = bq.at[0, c, B, A]
    own_o = bo.at[c, B, A, :, pl.ds(pl.multiple_of(384 * x, 128), 384)]
    qx = rc("qx", own_q, bq.at[1, c, B, A], dp, far)
    ox = [rc("ox%d" % d, own_o, own_o, dp, mod4(x + d)) for d in (1, 2, 3)]
    parts = [xg.at[x, :, pl.ds(0, 2 * D)], xg.at[x, :, pl.ds(2 * D, D)]]
    g1 = [rc("g1%d" % d, parts[0], parts[0], dp, mod4(x + d)) for d in (1, 2, 3)]
    g2 = [rc("g2%d" % d, parts[1], parts[1], dp, mod4(x + d)) for d in (1, 2, 3)]
    fn = rc("fn", nsend, nrm.at[x], dp, near)
    fm = rc("fm", nrm.at[x], nrm.at[x], dp, mate)
    fr = rc("fr", nrm.at[near], nrm.at[near], dp, mate)

    own_q[...] = w_qkv[...]
    own_o[...] = w_out[...]
    xg[x] = jnp.zeros((16, 3 * D), BF)
    xg[x, 0:12, 0 : 2 * D] = w_pw1[...]
    xg[x, 0:12, 2 * D :] = w_pw2[...]

    def split(i, carry):
        rows = pl.ds(pl.multiple_of(i * 48, 16), 48)
        v = raw[rows].astype(F32)
        for u in (0, 1):
            frames[u, rows, :] = v[:, u, :].astype(BF)
        return carry

    lax.fori_loop(0, L // 48, split, 0)
    pl.semaphore_wait(barrier, len(peers))
    qx.start()
    QA.P1()
    for copy in ox + g1 + g2:
        copy.start()

    def normed(u, target):
        def step(i, carry):
            rows = pl.ds(pl.multiple_of(i * ROWS, ROWS), ROWS)
            v = norm_rows(frames[u, rows, :].astype(F32), gain_a[...][None])
            target[rows, :] = v.astype(BF)
            return carry

        lax.fori_loop(0, L // ROWS, step, 0)

    normed(1 - a, nsend)
    fn.start()
    normed(a, nrm.at[x])
    fm.start()
    QA.P2()
    qx.wait_recv()
    QB.P1()
    length = lens[a]
    keys = lax.broadcasted_iota(jnp.int32, (T, 128), 0)
    lane = lax.broadcasted_iota(jnp.int32, (T, 128), 1)
    kbias[...] = jnp.where((keys >= length) & (lane == 0), -1e30, 0.0).astype(BF)
    QA.R2()
    QB.P2()
    for copy in ox:
        copy.wait_recv()
    O.P1()
    QA.S2()
    QB.R2()
    for copy in g1 + g2:
        copy.wait_recv()

    r = lax.broadcasted_iota(jnp.int32, (48, 64), 0)
    k = lax.broadcasted_iota(jnp.int32, (48, 64), 1)
    pick = ((lax.shift_right_logical(k, 4) * 12 + (k & 15) == r) & ((k & 15) < 12)).astype(F32).astype(BF)

    def assemble(first, count, target):
        for n in range(count):
            lanes = slice(768 * (first + n), 768 * (first + n) + 768)
            rows = jnp.concatenate([xg[i, :, lanes] for i in range(4)], axis=0)
            rows = jnp.dot(pick, rows, preferred_element_type=F32).astype(BF)
            target[c, B, A, :, 768 * n : 768 * n + 768] = rows

    assemble(0, 4, b1)
    assemble(4, 2, b2)
    W1.P1()
    W2.P1()
    O.R1()
    QA.F()
    QA.G()
    fn.wait_recv()
    fr.start()
    fm.wait_recv()

    def project(g, blocks):
        def step(m, carry):
            factor = jnp.where(m == 0, SCALE, 1.0).astype(F32)
            w = chunks(bq, slice(None), mat=(g, m))
            for j in blocks:
                rows = pl.ds(pl.multiple_of(j * L, 64), L)
                v = jnp.dot(nrm[j], w, preferred_element_type=F32)
                qkv[m, rows, 384 * g : 384 * g + 384] = (v * factor).astype(BF)
            return carry

        lax.fori_loop(0, 3, step, 0)

    project(0, (x, mate, near))
    QB.S2()
    QB.F()
    W1.R1()
    W2.R1()
    O.P2()
    QB.G()
    project(1, (x, mate, near))
    O.R2()
    W1.P2()
    fr.wait_recv()
    project(0, (far,))
    project(1, (far,))

    def send_pair(p, d):
        to = mod4(x + d)
        block = mod4(x + 2 * lax.div(p, 3))
        cols = pl.ds(pl.multiple_of(384 * block + 128 * lax.rem(p, 3), 128), 128)
        i = 94 + 3 * p + d - 1
        return pltpu.make_async_remote_copy(
            src_ref=ctxl.at[pl.ds(pl.multiple_of(to * L, L), L), pl.ds(pl.multiple_of(p * 128, 128), 128)],
            dst_ref=ctx.at[a, :, cols], send_sem=send.at[i], recv_sem=recv.at[i],
            device_id=(dp, to), device_id_type=pl.DeviceIdType.MESH,
        )

    half = lax.broadcasted_iota(jnp.int32, (QT, 128), 1) < HD

    def attend(p, carry):
        lanes = pl.ds(pl.multiple_of(p * 128, 128), 128)
        key = jnp.concatenate([qkv[1, :, lanes], kbias[...]], axis=1)
        value = jnp.concatenate([qkv[2, :, lanes], jnp.ones((T, 128), BF)], axis=1)

        def tile(j, carry):
            rows = pl.ds(pl.multiple_of(j * QT, QT), QT)
            q = qkv[0, rows, lanes]
            results = []
            for h in (0, 1):
                mine = jnp.where(half if h == 0 else ~half, q, jnp.zeros_like(q))
                query = jnp.concatenate([mine, jnp.ones((QT, 128), BF)], axis=1)
                s = lax.dot_general(
                    query, key, (((1,), (1,)), ((), ())), preferred_element_type=F32
                )
                e = jnp.exp2(s - jnp.max(s, -1, keepdims=True)).astype(BF)
                o = jnp.dot(e, value, preferred_element_type=F32)
                results.append(o[:, :128] / o[:, 128:])
            ctxl[rows, lanes] = jnp.where(half, results[0], results[1]).astype(BF)
            return carry

        lax.fori_loop(0, T // QT, tile, 0, unroll=T // QT)

        for d in (2, 1, 3):
            send_pair(p, d).start()

        @pl.when(p == 4)
        def _():
            W1.R2()
            W2.P2()
            O.S2()

        return carry

    lax.fori_loop(0, 6, attend, 0)
    O.F()
    for g in (0, 1):
        cols = pl.ds(pl.multiple_of(384 * mod4(x + 2 * g), 128), 384)
        ctx[a, :, cols] = ctxl[pl.ds(pl.multiple_of(x * L, L), L), 384 * g : 384 * g + 384]
    O.G()

    def arrive(p, carry):
        for d in (1, 2, 3):
            send_pair(p, d).wait_recv()
        return carry

    lax.fori_loop(0, 6, arrive, 0)

    for n in range(2):
        w = chunks(bo, slice(None), 16 * n, 16)
        cols = slice(768 * n, 768 * n + 768)
        att = lax.dot_general(
            ctx[...].reshape(2 * L, D), w, (((1,), (1,)), ((), ())), preferred_element_type=F32
        )
        total = frames[:, :, cols].astype(F32) + att.reshape(2, L, 768)
        res[:, :, cols] = total.astype(BF)

    def norm_conv(i, carry):
        u, rows = lax.div(i, L // ROWS), pl.ds(pl.multiple_of(lax.rem(i, L // ROWS) * ROWS, ROWS), ROWS)
        cin[u, rows, :] = norm_rows(res[u, rows, :].astype(F32), gain_c[...][None]).astype(BF)
        return carry

    lax.fori_loop(0, 2 * (L // ROWS), norm_conv, 0)
    W1.S2()
    W1.F()
    W1.G()
    time = x * L + lax.broadcasted_iota(jnp.int32, (L, 256), 0)

    halo = []
    for v in (0, 1):
        at = lambda row: gp.at[:, pl.ds(row, EDGE), pl.ds(768 * v, 768)]
        halo.append(rc("h+%d" % v, at(L), at(0), dp, mod4(x + 1)))
        halo.append(rc("h-%d" % v, at(EDGE), at(EDGE + L), dp, mod4(x + 3)))

    def glu(n, carry):
        lanes = pl.ds(pl.multiple_of(n * 256, 256), 256)
        wv = chunks(b1, lanes)
        wg = chunks(b1, pl.ds(pl.multiple_of(n * 256 + D, 256), 256))
        rows = cin[...].reshape(2 * L, D)
        v = jnp.dot(rows, wv, preferred_element_type=F32)
        g = jnp.dot(rows, wg, preferred_element_type=F32)
        v = (v * sigmoid(g)).reshape(2, L, 256)
        for u in (0, 1):
            gp[u, EDGE : EDGE + L, lanes] = jnp.where(time < lens[u], v[u], 0.0).astype(BF)

        @pl.when(n == 2)
        def _():
            halo[0].start()
            halo[1].start()

        @pl.when(n == 0)
        def _():
            W2.R2()

        return carry

    lax.fori_loop(0, 6, glu, 0)
    halo[2].start()
    halo[3].start()
    W2.S2()
    halo[0].wait_recv()
    halo[1].wait_recv()
    first = jnp.where(x == 0, 0.0, 1.0).astype(F32)
    last = jnp.where(x == 3, 0.0, 1.0).astype(F32)

    def conv(i, carry):
        u, n = lax.rem(i, 2), lax.div(i, 2)
        lanes = pl.ds(pl.multiple_of(n * 128, 128), 128)
        cf[0:EDGE, :] = gp[u, 0:EDGE, lanes].astype(F32) * first
        cf[EDGE : EDGE + L, :] = gp[u, EDGE : EDGE + L, lanes].astype(F32)
        cf[EDGE + L :, :] = gp[u, EDGE + L :, lanes].astype(F32) * last
        tap = taps[:, lanes]
        total = jnp.zeros((L, 128), F32)
        for k in range(KERNEL):
            total = total + cf[k + 1 : k + 1 + L, :] * tap[k : k + 1, :]
        dep[u, :, lanes] = total
        return carry

    lax.fori_loop(0, 12, conv, 0)
    halo[2].wait_recv()
    halo[3].wait_recv()
    lax.fori_loop(12, 24, conv, 0)
    W2.F()

    def norm_mid(i, carry):
        u, rows = lax.div(i, L // ROWS), pl.ds(pl.multiple_of(lax.rem(i, L // ROWS) * ROWS, ROWS), ROWS)
        h = norm_rows(dep[u, rows, :], gain_m[...][None])
        cin[u, rows, :] = (h * sigmoid(h)).astype(BF)
        return carry

    lax.fori_loop(0, 2 * (L // ROWS), norm_mid, 0)

    W2.G()

    def last_product(n, carry):
        lanes = pl.ds(pl.multiple_of(n * 256, 256), 256)
        w = chunks(b2, lanes)
        v = jnp.dot(cin[...].reshape(2 * L, D), w, preferred_element_type=F32).reshape(2, L, 256)
        for u in (0, 1):
            total = v[u] + res[u, :, lanes].astype(F32)
            out[u, :, lanes] = jnp.where(time < lens[u], total, 0.0).astype(BF)
        return carry

    lax.fori_loop(0, 6, last_product, 0)

    for ring in (QA, QB, O, W1, W2):
        ring.done()
    for copy in [qx] + ox + g1 + g2 + [fn, fm, fr] + halo:
        copy.wait_send()

    def leave(p, carry):
        for d in (1, 2, 3):
            send_pair(p, d).wait_send()
        return carry

    lax.fori_loop(0, 6, leave, 0)


def local(
    frames, lengths, attn_gain, w_qkv, w_out, conv_gain, w_pw1, depth_kernel, mid_gain, w_pw2
):
    vmem = pl.BlockSpec(memory_space=pltpu.VMEM)
    result = pl.pallas_call(
        body,
        out_shape=jax.ShapeDtypeStruct((2, L, D), BF),
        in_specs=[pl.BlockSpec(memory_space=pltpu.SMEM)] + [vmem] * 9,
        out_specs=vmem,
        scratch_shapes=[
            pltpu.VMEM((2, 2, 4, 4, 3, 48, 384), BF),
            pltpu.VMEM((2, 4, 4, 48, D), BF),
            pltpu.VMEM((2, 4, 4, 48, 2 * D), BF),
            pltpu.VMEM((2, 4, 4, 48, D), BF),
            pltpu.VMEM((4, 16, 3 * D), BF),
            pltpu.VMEM((4, L, D), BF),
            pltpu.VMEM((L, D), BF),
            pltpu.VMEM((3, T, 768), BF),
            pltpu.VMEM((T, 128), BF),
            pltpu.VMEM((T, 768), BF),
            pltpu.VMEM((2, L, D), BF),
            pltpu.VMEM((2, L, D), BF),
            pltpu.VMEM((2, L, D), BF),
            pltpu.VMEM((2, L + 2 * EDGE, D), BF),
            pltpu.VMEM((L + 2 * EDGE, 128), F32),
            pltpu.VMEM((2, L, D), F32),
            pltpu.VMEM((2, L, D), BF),
            pltpu.SemaphoreType.DMA((NSEM,)),
            pltpu.SemaphoreType.DMA((NSEM,)),
        ],
        compiler_params=pltpu.CompilerParams(
            collective_id=0, has_side_effects=True, vmem_limit_bytes=60 * 1024 * 1024
        ),
        name="layer",
    )(
        lengths, frames, attn_gain, w_qkv, w_out.T, conv_gain, w_pw1, w_pw2, depth_kernel, mid_gain,
    )
    return jnp.swapaxes(result, 0, 1)


def solution(mesh):
    in_specs = (
        P("seq", "dp", None),
        P("dp"),
        P(),
        P(None, "dp", "seq"),
        P("seq", "dp"),
        P(),
        P(("dp", "seq"), None),
        P(),
        P(),
        P(("dp", "seq"), None),
    )
    out_specs = P("seq", "dp", None)
    return jax.shard_map(local, mesh=mesh, in_specs=in_specs, out_specs=out_specs, check_vma=False)
```

```python
import functools

import jax
import jax.numpy as jnp
from jax import lax
from jax.experimental import pallas as pl
from jax.experimental.pallas import tpu as pltpu
from jax.sharding import PartitionSpec as P

HD = 64
KERNEL = 31
D = 1536
T = 768
L = 192
EDGE = 16
BF = jnp.bfloat16
F32 = jnp.float32
SCALE = 1.4426950408889634 / 8.0
NSEM = 112
QT = 384
ROWS = 192


def sigmoid(v):
    return 0.5 * jnp.tanh(0.5 * v) + 0.5


def norm_rows(v, gain):
    mean = jnp.mean(v, -1, keepdims=True)
    centred = v - mean
    spread = jnp.mean(centred * centred, -1, keepdims=True)
    return centred * lax.rsqrt(spread + 1e-05) * gain


def chunks(buf, lanes, first=0, count=32, mat=None):
    out = []
    for i in range(first, first + count):
        z, y, c = i // 8, (i // 2) % 4, i % 2
        where = (c, z, y) if c == 0 else (c, y, z)
        if mat is not None:
            where = (mat[0],) + where + (mat[1],)
        out.append(buf[where + (slice(None), lanes)])
    return jnp.concatenate(out, axis=0)


def body(
    lens, raw, gain_a, w_qkv, w_out, gain_c, w_pw1, w_pw2, taps, gain_m, out,
    bq, bo, b1, b2, xg, nrm, nsend, qkv, kbias, ctxl, ctx, res, cin, gp, cf, dep, frames, send, recv,
):
    x = lax.axis_index("seq")
    dp = lax.axis_index("dp")
    z, y, c = lax.div(dp, 8), lax.rem(lax.div(dp, 2), 4), lax.rem(dp, 2)

    def mod4(v):
        return lax.rem(v, 4)

    xc = mod4(x + c)
    a = lax.div(xc, 2)

    A = (1 - c) * y + c * z
    B = (1 - c) * z + c * y

    def dev(Bv, Av):
        return (1 - c) * (Bv * 8 + Av * 2) + c * (Av * 8 + Bv * 2 + 1)

    Ap, Am, Bp, Bm, Bf = mod4(A + 1), mod4(A + 3), mod4(B + 1), mod4(B + 3), mod4(B + 2)
    dAp, dAm, dBp, dBm = dev(B, Ap), dev(B, Am), dev(Bp, A), dev(Bm, A)
    dAf = dev(B, mod4(A + 2))
    sib = dp + 1 - 2 * c
    near, mate = mod4(7 - xc - c), mod4(xc + 5 - 2 * lax.rem(xc, 2) - c)
    far = mod4(x + 2)

    names = {}

    def rc(name, src, dst, to_dp, to_x):
        i = names.setdefault(name, len(names))
        return pltpu.make_async_remote_copy(
            src_ref=src, dst_ref=dst, send_sem=send.at[i], recv_sem=recv.at[i],
            device_id=(to_dp, to_x), device_id_type=pl.DeviceIdType.MESH,
        )

    barrier = pltpu.get_barrier_semaphore()
    peers = [(dp, mod4(x + d)) for d in (1, 2, 3)]
    peers += [(d, x) for d in (dAp, dAm, dAf, dBp, dBm, sib)]
    for peer in peers:
        pl.semaphore_signal(barrier, inc=1, device_id=peer, device_id_type=pl.DeviceIdType.MESH)

    class Ring:
        def __init__(self, key, buf, half, direct=False):
            same = lambda n, ref, to: rc(key + n, ref, ref, to, x)
            lo, hi_ = pl.ds(0, half), pl.ds(half, half)
            mid = (slice(None),) * (len(buf.shape) - 4)
            if direct:
                self.r1 = []
                self.p1 = [
                    same("p1" + m, buf.at[c, B, A], to)
                    for m, to in (("+", dAp), ("-", dAm), ("2", dAf))
                ]
            else:
                self.p1 = [same("p1+", buf.at[c, B, A], dAp), same("p1-", buf.at[c, B, A], dAm)]
                self.r1 = [
                    same("r1+", buf.at[(c, B, Am) + mid + (lo,)], dAp),
                    same("r1-", buf.at[(c, B, Ap) + mid + (hi_,)], dAm),
                ]
            first, second = pl.ds(0, 2), pl.ds(2, 2)
            self.p2 = [
                same("p2a+", buf.at[c, B, first], dBp), same("p2a-", buf.at[c, B, second], dBm),
                same("p2b+", buf.at[c, B, second], dBp), same("p2b-", buf.at[c, B, first], dBm),
            ]
            self.r2 = [
                same("r2+", buf.at[c, Bm, first], dBp), same("r2-", buf.at[c, Bp, second], dBm),
            ]
            self.s = [same("s%d" % i, buf.at[c, v], sib) for i, v in enumerate((B, Bm, Bp, Bf))]
            self.sent = self.p1 + self.r1 + self.p2 + self.r2 + self.s

        def P1(self):
            for copy in self.p1:
                copy.start()

        def R1(self):
            for i in (0, 1):
                self.p1[i].wait_recv()
                self.r1[i].start()

        def P2(self):
            for copy in self.r1 or self.p1:
                copy.wait_recv()
            for copy in self.p2:
                copy.start()
            self.s[0].start()

        def R2(self):
            for i in (0, 1):
                self.p2[i].wait_recv()
                self.r2[i].start()

        def S2(self):
            for i in (0, 1):
                self.p2[2 + i].wait_recv()
                self.s[1 + i].start()

        def F(self):
            self.r2[0].wait_recv()
            self.r2[1].wait_recv()
            self.s[3].start()

        def G(self):
            for copy in self.s:
                copy.wait_recv()

        def done(self):
            for copy in self.sent:
                copy.wait_send()

    QA, QB = Ring("q", bq.at[0], 0, True), Ring("r", bq.at[1], 0, True)
    O = Ring("o", bo, 768)
    W1, W2 = Ring("v", b1, 1536), Ring("w", b2, 768)

    own_q = bq.at[0, c, B, A]
    own_o = bo.at[c, B, A, :, pl.ds(pl.multiple_of(384 * x, 128), 384)]
    qx = rc("qx", own_q, bq.at[1, c, B, A], dp, far)
    ox = [rc("ox%d" % d, own_o, own_o, dp, mod4(x + d)) for d in (1, 2, 3)]
    parts = [xg.at[x, :, pl.ds(0, 2 * D)], xg.at[x, :, pl.ds(2 * D, D)]]
    g1 = [rc("g1%d" % d, parts[0], parts[0], dp, mod4(x + d)) for d in (1, 2, 3)]
    g2 = [rc("g2%d" % d, parts[1], parts[1], dp, mod4(x + d)) for d in (1, 2, 3)]
    fn = rc("fn", nsend, nrm.at[x], dp, near)
    fm = rc("fm", nrm.at[x], nrm.at[x], dp, mate)
    fr = rc("fr", nrm.at[near], nrm.at[near], dp, mate)

    own_q[...] = w_qkv[...]
    own_o[...] = w_out[...]
    xg[x] = jnp.zeros((16, 3 * D), BF)
    xg[x, 0:12, 0 : 2 * D] = w_pw1[...]
    xg[x, 0:12, 2 * D :] = w_pw2[...]

    pl.semaphore_wait(barrier, len(peers))
    qx.start()
    QA.P1()
    for copy in ox + g1 + g2:
        copy.start()

    def split(i, carry):
        rows = pl.ds(pl.multiple_of(i * 48, 16), 48)
        v = raw[rows].astype(F32)
        for u in (0, 1):
            frames[u, rows, :] = v[:, u, :].astype(BF)
        return carry

    lax.fori_loop(0, L // 48, split, 0)

    def normed(u, target):
        def step(i, carry):
            rows = pl.ds(pl.multiple_of(i * ROWS, ROWS), ROWS)
            v = norm_rows(frames[u, rows, :].astype(F32), gain_a[...][None])
            target[rows, :] = v.astype(BF)
            return carry

        lax.fori_loop(0, L // ROWS, step, 0)

    normed(1 - a, nsend)
    fn.start()
    normed(a, nrm.at[x])
    fm.start()
    QA.P2()
    qx.wait_recv()
    QB.P1()
    length = lens[a]
    keys = lax.broadcasted_iota(jnp.int32, (T, 128), 0)
    lane = lax.broadcasted_iota(jnp.int32, (T, 128), 1)
    kbias[...] = jnp.where((keys >= length) & (lane == 0), -1e30, 0.0).astype(BF)
    QA.R2()
    QB.P2()
    for copy in ox:
        copy.wait_recv()
    O.P1()
    QA.S2()
    QB.R2()
    for copy in g1 + g2:
        copy.wait_recv()

    r = lax.broadcasted_iota(jnp.int32, (48, 64), 0)
    k = lax.broadcasted_iota(jnp.int32, (48, 64), 1)
    pick = ((lax.shift_right_logical(k, 4) * 12 + (k & 15) == r) & ((k & 15) < 12)).astype(F32).astype(BF)

    def assemble(first, count, target):
        for n in range(count):
            lanes = slice(768 * (first + n), 768 * (first + n) + 768)
            rows = jnp.concatenate([xg[i, :, lanes] for i in range(4)], axis=0)
            rows = jnp.dot(pick, rows, preferred_element_type=F32).astype(BF)
            target[c, B, A, :, 768 * n : 768 * n + 768] = rows

    assemble(0, 4, b1)
    assemble(4, 2, b2)
    W1.P1()
    W2.P1()
    O.R1()
    QA.F()
    QA.G()
    fn.wait_recv()
    fr.start()
    fm.wait_recv()

    def project(g, blocks):
        def step(m, carry):
            factor = jnp.where(m == 0, SCALE, 1.0).astype(F32)
            w = chunks(bq, slice(None), mat=(g, m))
            for j in blocks:
                rows = pl.ds(pl.multiple_of(j * L, 64), L)
                v = jnp.dot(nrm[j], w, preferred_element_type=F32)
                qkv[m, rows, 384 * g : 384 * g + 384] = (v * factor).astype(BF)
            return carry

        lax.fori_loop(0, 3, step, 0)

    project(0, (x, mate, near))
    QB.S2()
    QB.F()
    W1.R1()
    W2.R1()
    O.P2()
    QB.G()
    project(1, (x, mate, near))
    O.R2()
    W1.P2()
    fr.wait_recv()
    project(0, (far,))
    project(1, (far,))

    def send_pair(p, d):
        to = mod4(x + d)
        block = mod4(x + 2 * lax.div(p, 3))
        cols = pl.ds(pl.multiple_of(384 * block + 128 * lax.rem(p, 3), 128), 128)
        i = 94 + 3 * p + d - 1
        return pltpu.make_async_remote_copy(
            src_ref=ctxl.at[pl.ds(pl.multiple_of(to * L, L), L), pl.ds(pl.multiple_of(p * 128, 128), 128)],
            dst_ref=ctx.at[a, :, cols], send_sem=send.at[i], recv_sem=recv.at[i],
            device_id=(dp, to), device_id_type=pl.DeviceIdType.MESH,
        )

    half = lax.broadcasted_iota(jnp.int32, (QT, 128), 1) < HD

    def attend(p, carry):
        lanes = pl.ds(pl.multiple_of(p * 128, 128), 128)
        key = jnp.concatenate([qkv[1, :, lanes], kbias[...]], axis=1)
        value = jnp.concatenate([qkv[2, :, lanes], jnp.ones((T, 128), BF)], axis=1)

        def tile(j, carry):
            rows = pl.ds(pl.multiple_of(j * QT, QT), QT)
            q = qkv[0, rows, lanes]
            results = []
            for h in (0, 1):
                mine = jnp.where(half if h == 0 else ~half, q, jnp.zeros_like(q))
                query = jnp.concatenate([mine, jnp.ones((QT, 128), BF)], axis=1)
                s = lax.dot_general(
                    query, key, (((1,), (1,)), ((), ())), preferred_element_type=F32
                )
                e = jnp.exp2(s - jnp.max(s, -1, keepdims=True)).astype(BF)
                o = jnp.dot(e, value, preferred_element_type=F32)
                results.append(o[:, :128] / o[:, 128:])
            ctxl[rows, lanes] = jnp.where(half, results[0], results[1]).astype(BF)
            return carry

        lax.fori_loop(0, T // QT, tile, 0, unroll=T // QT)

        for d in (2, 1, 3):
            send_pair(p, d).start()

        @pl.when(p == 4)
        def _():
            W1.R2()
            W2.P2()
            O.S2()

        return carry

    lax.fori_loop(0, 6, attend, 0)
    O.F()
    for g in (0, 1):
        cols = pl.ds(pl.multiple_of(384 * mod4(x + 2 * g), 128), 384)
        ctx[a, :, cols] = ctxl[pl.ds(pl.multiple_of(x * L, L), L), 384 * g : 384 * g + 384]
    O.G()

    def arrive(p, carry):
        for d in (1, 2, 3):
            send_pair(p, d).wait_recv()
        return carry

    lax.fori_loop(0, 6, arrive, 0)

    for n in range(2):
        w = chunks(bo, slice(None), 16 * n, 16)
        cols = slice(768 * n, 768 * n + 768)
        att = lax.dot_general(
            ctx[...].reshape(2 * L, D), w, (((1,), (1,)), ((), ())), preferred_element_type=F32
        )
        total = frames[:, :, cols].astype(F32) + att.reshape(2, L, 768)
        res[:, :, cols] = total.astype(BF)

    def norm_conv(i, carry):
        u, rows = lax.div(i, L // ROWS), pl.ds(pl.multiple_of(lax.rem(i, L // ROWS) * ROWS, ROWS), ROWS)
        cin[u, rows, :] = norm_rows(res[u, rows, :].astype(F32), gain_c[...][None]).astype(BF)
        return carry

    lax.fori_loop(0, 2 * (L // ROWS), norm_conv, 0)
    W1.S2()
    W1.F()
    W1.G()
    time = x * L + lax.broadcasted_iota(jnp.int32, (L, 256), 0)

    halo = []
    for v in (0, 1):
        at = lambda row: gp.at[:, pl.ds(row, EDGE), pl.ds(768 * v, 768)]
        halo.append(rc("h+%d" % v, at(L), at(0), dp, mod4(x + 1)))
        halo.append(rc("h-%d" % v, at(EDGE), at(EDGE + L), dp, mod4(x + 3)))

    def glu(n, carry):
        lanes = pl.ds(pl.multiple_of(n * 256, 256), 256)
        wv = chunks(b1, lanes)
        wg = chunks(b1, pl.ds(pl.multiple_of(n * 256 + D, 256), 256))
        rows = cin[...].reshape(2 * L, D)
        v = jnp.dot(rows, wv, preferred_element_type=F32)
        g = jnp.dot(rows, wg, preferred_element_type=F32)
        v = (v * sigmoid(g)).reshape(2, L, 256)
        for u in (0, 1):
            gp[u, EDGE : EDGE + L, lanes] = jnp.where(time < lens[u], v[u], 0.0).astype(BF)

        @pl.when(n == 2)
        def _():
            halo[0].start()
            halo[1].start()

        @pl.when(n == 0)
        def _():
            W2.R2()

        return carry

    lax.fori_loop(0, 6, glu, 0, unroll=2)
    halo[2].start()
    halo[3].start()
    W2.S2()
    halo[0].wait_recv()
    halo[1].wait_recv()
    first = jnp.where(x == 0, 0.0, 1.0).astype(F32)
    last = jnp.where(x == 3, 0.0, 1.0).astype(F32)

    def conv(i, carry):
        u, n = lax.rem(i, 2), lax.div(i, 2)
        lanes = pl.ds(pl.multiple_of(n * 128, 128), 128)
        cf[0:EDGE, :] = gp[u, 0:EDGE, lanes].astype(F32) * first
        cf[EDGE : EDGE + L, :] = gp[u, EDGE : EDGE + L, lanes].astype(F32)
        cf[EDGE + L :, :] = gp[u, EDGE + L :, lanes].astype(F32) * last
        tap = taps[:, lanes]
        total = jnp.zeros((L, 128), F32)
        for k in range(KERNEL):
            total = total + cf[k + 1 : k + 1 + L, :] * tap[k : k + 1, :]
        dep[u, :, lanes] = total
        return carry

    lax.fori_loop(0, 12, conv, 0, unroll=2)
    halo[2].wait_recv()
    halo[3].wait_recv()
    lax.fori_loop(12, 24, conv, 0, unroll=2)
    W2.F()

    def norm_mid(i, carry):
        u, rows = lax.div(i, L // ROWS), pl.ds(pl.multiple_of(lax.rem(i, L // ROWS) * ROWS, ROWS), ROWS)
        h = norm_rows(dep[u, rows, :], gain_m[...][None])
        cin[u, rows, :] = (h * sigmoid(h)).astype(BF)
        return carry

    lax.fori_loop(0, 2 * (L // ROWS), norm_mid, 0)

    W2.G()

    def last_product(n, carry):
        lanes = pl.ds(pl.multiple_of(n * 256, 256), 256)
        w = chunks(b2, lanes)
        v = jnp.dot(cin[...].reshape(2 * L, D), w, preferred_element_type=F32).reshape(2, L, 256)
        for u in (0, 1):
            total = v[u] + res[u, :, lanes].astype(F32)
            out[u, :, lanes] = jnp.where(time < lens[u], total, 0.0).astype(BF)
        return carry

    lax.fori_loop(0, 6, last_product, 0, unroll=2)

    for ring in (QA, QB, O, W1, W2):
        ring.done()
    for copy in [qx] + ox + g1 + g2 + [fn, fm, fr] + halo:
        copy.wait_send()

    def leave(p, carry):
        for d in (1, 2, 3):
            send_pair(p, d).wait_send()
        return carry

    lax.fori_loop(0, 6, leave, 0)


def local(
    frames, lengths, attn_gain, w_qkv, w_out, conv_gain, w_pw1, depth_kernel, mid_gain, w_pw2
):
    vmem = pl.BlockSpec(memory_space=pltpu.VMEM)
    result = pl.pallas_call(
        body,
        out_shape=jax.ShapeDtypeStruct((2, L, D), BF),
        in_specs=[pl.BlockSpec(memory_space=pltpu.SMEM)] + [vmem] * 9,
        out_specs=vmem,
        scratch_shapes=[
            pltpu.VMEM((2, 2, 4, 4, 3, 48, 384), BF),
            pltpu.VMEM((2, 4, 4, 48, D), BF),
            pltpu.VMEM((2, 4, 4, 48, 2 * D), BF),
            pltpu.VMEM((2, 4, 4, 48, D), BF),
            pltpu.VMEM((4, 16, 3 * D), BF),
            pltpu.VMEM((4, L, D), BF),
            pltpu.VMEM((L, D), BF),
            pltpu.VMEM((3, T, 768), BF),
            pltpu.VMEM((T, 128), BF),
            pltpu.VMEM((T, 768), BF),
            pltpu.VMEM((2, L, D), BF),
            pltpu.VMEM((2, L, D), BF),
            pltpu.VMEM((2, L, D), BF),
            pltpu.VMEM((2, L + 2 * EDGE, D), BF),
            pltpu.VMEM((L + 2 * EDGE, 128), F32),
            pltpu.VMEM((2, L, D), F32),
            pltpu.VMEM((2, L, D), BF),
            pltpu.SemaphoreType.DMA((NSEM,)),
            pltpu.SemaphoreType.DMA((NSEM,)),
        ],
        compiler_params=pltpu.CompilerParams(
            collective_id=0, has_side_effects=True, vmem_limit_bytes=60 * 1024 * 1024
        ),
        name="layer",
    )(
        lengths, frames, attn_gain, w_qkv, w_out.T, conv_gain, w_pw1, w_pw2, depth_kernel, mid_gain,
    )
    return jnp.swapaxes(result, 0, 1)


def solution(mesh):
    in_specs = (
        P("seq", "dp", None),
        P("dp"),
        P(),
        P(None, "dp", "seq"),
        P("seq", "dp"),
        P(),
        P(("dp", "seq"), None),
        P(),
        P(),
        P(("dp", "seq"), None),
    )
    out_specs = P("seq", "dp", None)
    return jax.shard_map(local, mesh=mesh, in_specs=in_specs, out_specs=out_specs, check_vma=False)
```

```python
import functools

import jax
import jax.numpy as jnp
from jax import lax
from jax.experimental import pallas as pl
from jax.experimental.pallas import tpu as pltpu
from jax.sharding import PartitionSpec as P

HD = 64
KERNEL = 31
D = 1536
T = 768
L = 192
EDGE = 16
BF = jnp.bfloat16
F32 = jnp.float32
SCALE = 1.4426950408889634 / 8.0
NSEM = 112
QT = 384
ROWS = 192


def sigmoid(v):
    return 0.5 * jnp.tanh(0.5 * v) + 0.5


def norm_rows(v, gain):
    mean = jnp.mean(v, -1, keepdims=True)
    centred = v - mean
    spread = jnp.mean(centred * centred, -1, keepdims=True)
    return centred * lax.rsqrt(spread + 1e-05) * gain


def chunks(buf, lanes, first=0, count=32, mat=None):
    out = []
    for i in range(first, first + count):
        z, y, c = i // 8, (i // 2) % 4, i % 2
        where = (c, z, y) if c == 0 else (c, y, z)
        if mat is not None:
            where = (mat[0],) + where + (mat[1],)
        out.append(buf[where + (slice(None), lanes)])
    return jnp.concatenate(out, axis=0)


def body(
    lens, raw, gain_a, w_qkv, w_out, gain_c, w_pw1, w_pw2, taps, gain_m, out,
    bq, bo, b1, b2, xg, nrm, nsend, qkv, kbias, ctxl, ctx, res, cin, gp, cf, dep, frames, send, recv,
):
    x = lax.axis_index("seq")
    dp = lax.axis_index("dp")
    z, y, c = lax.div(dp, 8), lax.rem(lax.div(dp, 2), 4), lax.rem(dp, 2)

    def mod4(v):
        return lax.rem(v, 4)

    xc = mod4(x + c)
    a = lax.div(xc, 2)

    A = (1 - c) * y + c * z
    B = (1 - c) * z + c * y

    def dev(Bv, Av):
        return (1 - c) * (Bv * 8 + Av * 2) + c * (Av * 8 + Bv * 2 + 1)

    Ap, Am, Bp, Bm, Bf = mod4(A + 1), mod4(A + 3), mod4(B + 1), mod4(B + 3), mod4(B + 2)
    dAp, dAm, dBp, dBm = dev(B, Ap), dev(B, Am), dev(Bp, A), dev(Bm, A)
    dAf = dev(B, mod4(A + 2))
    sib = dp + 1 - 2 * c
    near, mate = mod4(7 - xc - c), mod4(xc + 5 - 2 * lax.rem(xc, 2) - c)
    far = mod4(x + 2)

    names = {}

    def rc(name, src, dst, to_dp, to_x):
        i = names.setdefault(name, len(names))
        return pltpu.make_async_remote_copy(
            src_ref=src, dst_ref=dst, send_sem=send.at[i], recv_sem=recv.at[i],
            device_id=(to_dp, to_x), device_id_type=pl.DeviceIdType.MESH,
        )

    barrier = pltpu.get_barrier_semaphore()
    peers = [(dp, mod4(x + d)) for d in (1, 2, 3)]
    peers += [(d, x) for d in (dAp, dAm, dAf, dBp, dBm, sib)]
    for peer in peers:
        pl.semaphore_signal(barrier, inc=1, device_id=peer, device_id_type=pl.DeviceIdType.MESH)

    class Ring:
        def __init__(self, key, buf, half, direct=False):
            same = lambda n, ref, to: rc(key + n, ref, ref, to, x)
            lo, hi_ = pl.ds(0, half), pl.ds(half, half)
            mid = (slice(None),) * (len(buf.shape) - 4)
            if direct:
                self.r1 = []
                self.p1 = [
                    same("p1" + m, buf.at[c, B, A], to)
                    for m, to in (("+", dAp), ("-", dAm), ("2", dAf))
                ]
            else:
                self.p1 = [same("p1+", buf.at[c, B, A], dAp), same("p1-", buf.at[c, B, A], dAm)]
                self.r1 = [
                    same("r1+", buf.at[(c, B, Am) + mid + (lo,)], dAp),
                    same("r1-", buf.at[(c, B, Ap) + mid + (hi_,)], dAm),
                ]
            first, second = pl.ds(0, 2), pl.ds(2, 2)
            self.p2 = [
                same("p2a+", buf.at[c, B, first], dBp), same("p2a-", buf.at[c, B, second], dBm),
                same("p2b+", buf.at[c, B, second], dBp), same("p2b-", buf.at[c, B, first], dBm),
            ]
            self.r2 = [
                same("r2+", buf.at[c, Bm, first], dBp), same("r2-", buf.at[c, Bp, second], dBm),
            ]
            self.s = [same("s%d" % i, buf.at[c, v], sib) for i, v in enumerate((B, Bm, Bp, Bf))]
            self.sent = self.p1 + self.r1 + self.p2 + self.r2 + self.s

        def P1(self):
            for copy in self.p1:
                copy.start()

        def R1(self):
            for i in (0, 1):
                self.p1[i].wait_recv()
                self.r1[i].start()

        def P2(self):
            for copy in self.r1 or self.p1:
                copy.wait_recv()
            for copy in self.p2:
                copy.start()
            self.s[0].start()

        def R2(self):
            for i in (0, 1):
                self.p2[i].wait_recv()
                self.r2[i].start()

        def S2(self):
            for i in (0, 1):
                self.p2[2 + i].wait_recv()
                self.s[1 + i].start()

        def F(self):
            self.r2[0].wait_recv()
            self.r2[1].wait_recv()
            self.s[3].start()

        def G(self):
            for copy in self.s:
                copy.wait_recv()

        def done(self):
            for copy in self.sent:
                copy.wait_send()

    QA, QB = Ring("q", bq.at[0], 0, True), Ring("r", bq.at[1], 0, True)
    O = Ring("o", bo, 768)
    W1, W2 = Ring("v", b1, 1536), Ring("w", b2, 768)

    own_q = bq.at[0, c, B, A]
    own_o = bo.at[c, B, A, :, pl.ds(pl.multiple_of(384 * x, 128), 384)]
    qx = rc("qx", own_q, bq.at[1, c, B, A], dp, far)
    ox = [rc("ox%d" % d, own_o, own_o, dp, mod4(x + d)) for d in (1, 2, 3)]
    parts = [xg.at[x, :, pl.ds(0, 2 * D)], xg.at[x, :, pl.ds(2 * D, D)]]
    g1 = [rc("g1%d" % d, parts[0], parts[0], dp, mod4(x + d)) for d in (1, 2, 3)]
    g2 = [rc("g2%d" % d, parts[1], parts[1], dp, mod4(x + d)) for d in (1, 2, 3)]
    fn = rc("fn", nsend, nrm.at[x], dp, near)
    fm = rc("fm", nrm.at[x], nrm.at[x], dp, mate)
    fr = rc("fr", nrm.at[near], nrm.at[near], dp, mate)

    own_q[...] = w_qkv[...]
    own_o[...] = w_out[...]
    xg[x] = jnp.zeros((16, 3 * D), BF)
    xg[x, 0:12, 0 : 2 * D] = w_pw1[...]
    xg[x, 0:12, 2 * D :] = w_pw2[...]

    pl.semaphore_wait(barrier, len(peers))
    qx.start()
    QA.P1()
    for copy in ox + g1 + g2:
        copy.start()

    def split(i, carry):
        rows = pl.ds(pl.multiple_of(i * 48, 16), 48)
        v = raw[rows].astype(F32)
        for u in (0, 1):
            frames[u, rows, :] = v[:, u, :].astype(BF)
        return carry

    lax.fori_loop(0, L // 48, split, 0)

    def normed(u, target):
        def step(i, carry):
            rows = pl.ds(pl.multiple_of(i * ROWS, ROWS), ROWS)
            v = norm_rows(frames[u, rows, :].astype(F32), gain_a[...][None])
            target[rows, :] = v.astype(BF)
            return carry

        lax.fori_loop(0, L // ROWS, step, 0)

    normed(1 - a, nsend)
    fn.start()
    normed(a, nrm.at[x])
    fm.start()
    QA.P2()
    qx.wait_recv()
    QB.P1()
    length = lens[a]
    keys = lax.broadcasted_iota(jnp.int32, (T, 128), 0)
    lane = lax.broadcasted_iota(jnp.int32, (T, 128), 1)
    kbias[...] = jnp.where((keys >= length) & (lane == 0), -1e30, 0.0).astype(BF)
    QA.R2()
    QB.P2()
    for copy in ox:
        copy.wait_recv()
    O.P1()
    QA.S2()
    QB.R2()
    for copy in g1 + g2:
        copy.wait_recv()

    r = lax.broadcasted_iota(jnp.int32, (48, 64), 0)
    k = lax.broadcasted_iota(jnp.int32, (48, 64), 1)
    pick = ((lax.shift_right_logical(k, 4) * 12 + (k & 15) == r) & ((k & 15) < 12)).astype(F32).astype(BF)

    def assemble(first, count, target):
        for n in range(count):
            lanes = slice(768 * (first + n), 768 * (first + n) + 768)
            rows = jnp.concatenate([xg[i, :, lanes] for i in range(4)], axis=0)
            rows = jnp.dot(pick, rows, preferred_element_type=F32).astype(BF)
            target[c, B, A, :, 768 * n : 768 * n + 768] = rows

    assemble(0, 4, b1)
    assemble(4, 2, b2)
    W1.P1()
    W2.P1()
    O.R1()
    QA.F()
    QA.G()
    fn.wait_recv()
    fr.start()
    fm.wait_recv()

    def project(g, blocks):
        def step(m, carry):
            factor = jnp.where(m == 0, SCALE, 1.0).astype(F32)
            w = chunks(bq, slice(None), mat=(g, m))
            for j in blocks:
                rows = pl.ds(pl.multiple_of(j * L, 64), L)
                v = jnp.dot(nrm[j], w, preferred_element_type=F32)
                qkv[m, rows, 384 * g : 384 * g + 384] = (v * factor).astype(BF)
            return carry

        lax.fori_loop(0, 3, step, 0)

    project(0, (x, mate, near))
    QB.S2()
    QB.F()
    W1.R1()
    W2.R1()
    O.P2()
    QB.G()
    project(1, (x, mate, near))
    O.R2()
    W1.P2()
    fr.wait_recv()
    project(0, (far,))
    project(1, (far,))

    def send_pair(p, d):
        to = mod4(x + d)
        block = mod4(x + 2 * lax.div(p, 3))
        cols = pl.ds(pl.multiple_of(384 * block + 128 * lax.rem(p, 3), 128), 128)
        i = 94 + 3 * p + d - 1
        return pltpu.make_async_remote_copy(
            src_ref=ctxl.at[pl.ds(pl.multiple_of(to * L, L), L), pl.ds(pl.multiple_of(p * 128, 128), 128)],
            dst_ref=ctx.at[a, :, cols], send_sem=send.at[i], recv_sem=recv.at[i],
            device_id=(dp, to), device_id_type=pl.DeviceIdType.MESH,
        )

    half = lax.broadcasted_iota(jnp.int32, (QT, 128), 1) < HD

    def attend(p, carry):
        lanes = pl.ds(pl.multiple_of(p * 128, 128), 128)
        key = jnp.concatenate([qkv[1, :, lanes], kbias[...]], axis=1)
        value = jnp.concatenate([qkv[2, :, lanes], jnp.ones((T, 128), BF)], axis=1)

        def tile(j, carry):
            rows = pl.ds(pl.multiple_of(j * QT, QT), QT)
            q = qkv[0, rows, lanes]
            results = []
            for h in (0, 1):
                mine = jnp.where(half if h == 0 else ~half, q, jnp.zeros_like(q))
                query = jnp.concatenate([mine, jnp.ones((QT, 128), BF)], axis=1)
                s = lax.dot_general(
                    query, key, (((1,), (1,)), ((), ())), preferred_element_type=F32
                )
                e = jnp.exp2(s - jnp.max(s, -1, keepdims=True)).astype(BF)
                o = jnp.dot(e, value, preferred_element_type=F32)
                results.append(o[:, :128] / o[:, 128:])
            ctxl[rows, lanes] = jnp.where(half, results[0], results[1]).astype(BF)
            return carry

        lax.fori_loop(0, T // QT, tile, 0, unroll=T // QT)

        for d in (2, 1, 3):
            send_pair(p, d).start()

        @pl.when(p == 4)
        def _():
            W1.R2()
            W2.P2()
            O.S2()

        return carry

    lax.fori_loop(0, 6, attend, 0, unroll=2)
    O.F()
    for g in (0, 1):
        cols = pl.ds(pl.multiple_of(384 * mod4(x + 2 * g), 128), 384)
        ctx[a, :, cols] = ctxl[pl.ds(pl.multiple_of(x * L, L), L), 384 * g : 384 * g + 384]
    O.G()

    def arrive(p, carry):
        for d in (1, 2, 3):
            send_pair(p, d).wait_recv()
        return carry

    lax.fori_loop(0, 6, arrive, 0)

    for n in range(2):
        w = chunks(bo, slice(None), 16 * n, 16)
        cols = slice(768 * n, 768 * n + 768)
        att = lax.dot_general(
            ctx[...].reshape(2 * L, D), w, (((1,), (1,)), ((), ())), preferred_element_type=F32
        )
        total = frames[:, :, cols].astype(F32) + att.reshape(2, L, 768)
        res[:, :, cols] = total.astype(BF)

    def norm_conv(i, carry):
        u, rows = lax.div(i, L // ROWS), pl.ds(pl.multiple_of(lax.rem(i, L // ROWS) * ROWS, ROWS), ROWS)
        cin[u, rows, :] = norm_rows(res[u, rows, :].astype(F32), gain_c[...][None]).astype(BF)
        return carry

    lax.fori_loop(0, 2 * (L // ROWS), norm_conv, 0)
    W1.S2()
    W1.F()
    W1.G()
    time = x * L + lax.broadcasted_iota(jnp.int32, (L, 256), 0)

    halo = []
    for v in (0, 1):
        at = lambda row: gp.at[:, pl.ds(row, EDGE), pl.ds(768 * v, 768)]
        halo.append(rc("h+%d" % v, at(L), at(0), dp, mod4(x + 1)))
        halo.append(rc("h-%d" % v, at(EDGE), at(EDGE + L), dp, mod4(x + 3)))

    def glu(n, carry):
        lanes = pl.ds(pl.multiple_of(n * 256, 256), 256)
        wv = chunks(b1, lanes)
        wg = chunks(b1, pl.ds(pl.multiple_of(n * 256 + D, 256), 256))
        rows = cin[...].reshape(2 * L, D)
        v = jnp.dot(rows, wv, preferred_element_type=F32)
        g = jnp.dot(rows, wg, preferred_element_type=F32)
        v = (v * sigmoid(g)).reshape(2, L, 256)
        for u in (0, 1):
            gp[u, EDGE : EDGE + L, lanes] = jnp.where(time < lens[u], v[u], 0.0).astype(BF)

        @pl.when(n == 2)
        def _():
            halo[0].start()
            halo[1].start()

        @pl.when(n == 0)
        def _():
            W2.R2()

        return carry

    lax.fori_loop(0, 6, glu, 0, unroll=2)
    halo[2].start()
    halo[3].start()
    W2.S2()
    halo[0].wait_recv()
    halo[1].wait_recv()
    first = jnp.where(x == 0, 0.0, 1.0).astype(F32)
    last = jnp.where(x == 3, 0.0, 1.0).astype(F32)

    def conv(i, carry):
        u, n = lax.rem(i, 2), lax.div(i, 2)
        lanes = pl.ds(pl.multiple_of(n * 128, 128), 128)
        cf[0:EDGE, :] = gp[u, 0:EDGE, lanes].astype(F32) * first
        cf[EDGE : EDGE + L, :] = gp[u, EDGE : EDGE + L, lanes].astype(F32)
        cf[EDGE + L :, :] = gp[u, EDGE + L :, lanes].astype(F32) * last
        tap = taps[:, lanes]
        total = jnp.zeros((L, 128), F32)
        for k in range(KERNEL):
            total = total + cf[k + 1 : k + 1 + L, :] * tap[k : k + 1, :]
        dep[u, :, lanes] = total
        return carry

    lax.fori_loop(0, 12, conv, 0, unroll=2)
    halo[2].wait_recv()
    halo[3].wait_recv()
    lax.fori_loop(12, 24, conv, 0, unroll=2)
    W2.F()

    def norm_mid(i, carry):
        u, rows = lax.div(i, L // ROWS), pl.ds(pl.multiple_of(lax.rem(i, L // ROWS) * ROWS, ROWS), ROWS)
        h = norm_rows(dep[u, rows, :], gain_m[...][None])
        cin[u, rows, :] = (h * sigmoid(h)).astype(BF)
        return carry

    lax.fori_loop(0, 2 * (L // ROWS), norm_mid, 0)

    W2.G()

    def last_product(n, carry):
        lanes = pl.ds(pl.multiple_of(n * 256, 256), 256)
        w = chunks(b2, lanes)
        v = jnp.dot(cin[...].reshape(2 * L, D), w, preferred_element_type=F32).reshape(2, L, 256)
        for u in (0, 1):
            total = v[u] + res[u, :, lanes].astype(F32)
            out[u, :, lanes] = jnp.where(time < lens[u], total, 0.0).astype(BF)
        return carry

    lax.fori_loop(0, 6, last_product, 0, unroll=2)

    for ring in (QA, QB, O, W1, W2):
        ring.done()
    for copy in [qx] + ox + g1 + g2 + [fn, fm, fr] + halo:
        copy.wait_send()

    def leave(p, carry):
        for d in (1, 2, 3):
            send_pair(p, d).wait_send()
        return carry

    lax.fori_loop(0, 6, leave, 0)


def local(
    frames, lengths, attn_gain, w_qkv, w_out, conv_gain, w_pw1, depth_kernel, mid_gain, w_pw2
):
    vmem = pl.BlockSpec(memory_space=pltpu.VMEM)
    result = pl.pallas_call(
        body,
        out_shape=jax.ShapeDtypeStruct((2, L, D), BF),
        in_specs=[pl.BlockSpec(memory_space=pltpu.SMEM)] + [vmem] * 9,
        out_specs=vmem,
        scratch_shapes=[
            pltpu.VMEM((2, 2, 4, 4, 3, 48, 384), BF),
            pltpu.VMEM((2, 4, 4, 48, D), BF),
            pltpu.VMEM((2, 4, 4, 48, 2 * D), BF),
            pltpu.VMEM((2, 4, 4, 48, D), BF),
            pltpu.VMEM((4, 16, 3 * D), BF),
            pltpu.VMEM((4, L, D), BF),
            pltpu.VMEM((L, D), BF),
            pltpu.VMEM((3, T, 768), BF),
            pltpu.VMEM((T, 128), BF),
            pltpu.VMEM((T, 768), BF),
            pltpu.VMEM((2, L, D), BF),
            pltpu.VMEM((2, L, D), BF),
            pltpu.VMEM((2, L, D), BF),
            pltpu.VMEM((2, L + 2 * EDGE, D), BF),
            pltpu.VMEM((L + 2 * EDGE, 128), F32),
            pltpu.VMEM((2, L, D), F32),
            pltpu.VMEM((2, L, D), BF),
            pltpu.SemaphoreType.DMA((NSEM,)),
            pltpu.SemaphoreType.DMA((NSEM,)),
        ],
        compiler_params=pltpu.CompilerParams(
            collective_id=0, has_side_effects=True, vmem_limit_bytes=60 * 1024 * 1024
        ),
        name="layer",
    )(
        lengths, frames, attn_gain, w_qkv, w_out.T, conv_gain, w_pw1, w_pw2, depth_kernel, mid_gain,
    )
    return jnp.swapaxes(result, 0, 1)


def solution(mesh):
    in_specs = (
        P("seq", "dp", None),
        P("dp"),
        P(),
        P(None, "dp", "seq"),
        P("seq", "dp"),
        P(),
        P(("dp", "seq"), None),
        P(),
        P(),
        P(("dp", "seq"), None),
    )
    out_specs = P("seq", "dp", None)
    return jax.shard_map(local, mesh=mesh, in_specs=in_specs, out_specs=out_specs, check_vma=False)
```
